32 devices in a mesh: cell: 8 (over z, core), sub: 4 (over y, x).
Axes of the slice: x: 2, y: 2, z: 4, core: 2. Of those that a mesh axis runs over, the one named last changes fastest.
Arguments:
- queries: bfloat16 [2048, 1024], P('cell', 'sub'), may hold values from -384 to 384
- probe_groups: int32 [2048, 2], P('cell'), may hold values from 0 to 7, all different within a row; in each aligned block of 256 rows (0 to 255, 256 to 511, ...) at most 64 rows name the same one
- probe_cells: int32 [2048, 2, 16], P('cell'), may hold values from 0 to 31, as said below
- coarse: bfloat16 [256, 1024], P('cell', 'sub'), may hold values from -1.1953125 to 1.1953125
- codebooks: bfloat16 [64, 16, 256], P('sub'), may hold values from -1.5 to 1.5
- codes: int32 [256, 64, 384], P('cell', 'sub'), may hold values from 0 to 255
- lengths: int32 [256], P('cell'), may hold values from 1 to 384, 49152 in all
- payload: bfloat16 [256, 384, 256], P('cell', 'sub'), may hold values from -6 to 6
Outputs:
- pooled: bfloat16 [2048, 256], P('cell')
The draws below stay inside these ranges and needn't reach their ends.
Inputs may be any that keep to these rules, and one draw needn't show every extreme that they name: `probe_cells`: the 16 cells of one query in one group are distinct. `probe_groups`: the queries of one index of cell name one group at most 64 times, and one group exactly 64 times in some index. `lengths`: some cell has all 384 rows live.
All inputs are finite; a program needn't handle non-finite values. No bound on the sum of `lengths` on one device may be relied on, other than what follows from the above.
Results may differ from the reference program's by a relative error of at most 0.003.
The reference program's roundings to bfloat16 on the way count: a program that leaves them out, or rounds other values in their place, can miss the bound.
Values may be sent and summed in bfloat16 or wider, within the bound.
A program may use at most 64 MiB of HBM per device.

```python
import math
import jax
import jax.numpy as jnp
import numpy as np
from jax import lax

M = 64
SD = 16
K = 256
PW = 256
HALF = 16
CELL_DEV = 32
ROWS = 384
Q_DEV = 256
CAP = 64
DIM = 1024
QUERIES = 2048
CELLS = 256
N_CELL = 8


def draw_queries(key, part):
    base = jnp.clip(jax.random.normal(key, (QUERIES, DIM), jnp.float32), -6.0, 6.0)
    return base.astype(jnp.bfloat16)


def draw_probe_cells(key, part):
    keys = jax.random.split(key, QUERIES * 2)
    picks = jax.vmap(lambda single: jax.random.permutation(single, CELL_DEV)[:HALF])(keys)
    return picks.reshape(QUERIES, 2, HALF).astype(jnp.int32)


def place_ends(array, key, least, top_value):
    spot = [jax.random.randint(jax.random.fold_in(key, axis), (), 0, length) for axis, length in enumerate(array.shape)]
    widest = array.shape.index(max(array.shape))
    beside = spot[:widest] + [(spot[widest] + 1) % array.shape[widest]] + spot[widest + 1:]
    return array.at[tuple(spot)].set(least).at[tuple(beside)].set(top_value)


def shard_levels(own_key, dims, cuts, low, top_value):
    def one(axis_at, blocks):
        steps = jax.random.uniform(jax.random.fold_in(jax.random.fold_in(own_key, 6), axis_at), (blocks,), jnp.float32, low / len(cuts), top_value / len(cuts))
        return jnp.repeat(jnp.exp(steps), dims[axis_at] // blocks).reshape((-1,) + (1,) * (len(dims) - axis_at - 1))

    gain = one(*cuts[0])
    for cut in cuts[1:]:
        gain = gain * one(*cut)
    return gain


def profile(amount, total, bound, slope):
    portions = [(1 << 20) // math.isqrt(rank ** slope) + 1 for rank in range(2, amount + 1)]
    spare, given = total - bound - (amount - 1), [1] * (amount - 1)
    while spare > 0:
        free = [i for i in range(amount - 1) if given[i] < bound]
        whole, left = sum([portions[i] for i in free]), spare
        for i in free:
            addition = min(bound - given[i], max(1, left * portions[i] // whole), spare)
            given[i] = given[i] + addition
            spare = spare - addition
    return np.array([bound] + given)


def uneven_parts(stream_key, number_of, total, most, skew):
    if number_of == 2:
        one = jax.random.randint(stream_key, (), max(1, total - most), min(most, total - 1) + 1)
        return jnp.stack([one, total - one])
    sizes = jnp.asarray(profile(number_of, total, most, skew), jnp.int32)
    couples = (number_of - 1) // 2
    source_of, sink = sizes[1:1 + 2 * couples:2], sizes[2:2 + 2 * couples:2]
    slack = jnp.minimum(source_of - 1, most - sink)
    passed = jax.random.randint(jax.random.fold_in(stream_key, 1), (couples,), 0, 1 << 20) % (slack + 1)
    sizes = sizes.at[1:1 + 2 * couples:2].set(source_of - passed).at[2:2 + 2 * couples:2].set(sink + passed)
    return sizes[jax.random.permutation(jax.random.fold_in(stream_key, 2), number_of)]


def routed_block(own_key, own, number, rows, amount, top, most, skew):
    ranking = jax.random.permutation(own_key, amount)
    crowded, ordinary = portions_of(amount, rows * top, most, skew, True), portions_of(amount, rows * top, most, skew, False)
    places = jnp.arange(amount)

    def named(sizes, offset_by):
        used = int((sizes > 0).sum())
        fixed = max(1, used // 4)
        shifted = fixed + (places - fixed + offset_by * (used - fixed)) % max(1, amount - fixed)
        return jnp.zeros((amount,), jnp.int32).at[ranking[jnp.where(places < fixed, places, shifted)]].set(jnp.asarray(sizes, jnp.int32))

    sizes = jnp.where(number % 4 == 0, named(crowded, number // 4), named(ordinary, number - number // 4 - 1))
    mixed = jax.random.permutation(jax.random.fold_in(own, 3), amount)
    donor, taker = mixed[0:amount // 2 * 2:2], mixed[1:amount // 2 * 2:2]
    room = jnp.minimum(sizes[donor] - 1, most - sizes[taker]) // 2
    room = jnp.where((donor == ranking[0]) | (taker == ranking[0]) | (sizes[taker] == 0), 0, jnp.maximum(room, 0))
    shifted = jax.random.randint(jax.random.fold_in(own, 4), (amount // 2,), 0, 1 << 20) % (room + 1)
    sizes = sizes.at[donor].add(-shifted).at[taker].add(shifted)
    items = jnp.searchsorted(jnp.cumsum(sizes), jnp.arange(rows * top), side="right").astype(jnp.int32)
    grid = items.reshape(top, rows).T
    grid = grid[jax.random.permutation(jax.random.fold_in(own, 1), rows)]
    offset_by = jax.random.randint(jax.random.fold_in(own, 2), (rows, 1), 0, top)
    return jnp.take_along_axis(grid, (jnp.arange(top)[None, :] + offset_by) % top, axis=1)


def portions_of(number_of, total, most, lean, full):
    portions = [(1 << 20) // math.isqrt(standing ** lean) + 1 for standing in range(1, number_of + 1)]
    largest = most if full else min(most, max(-(-total // number_of), total * portions[0] // sum(portions)))
    least = 1 if total - largest >= number_of - 1 else 0
    holding, surplus = [largest] + [least] * (number_of - 1), total - largest - least * (number_of - 1)
    while surplus > 0:
        candidates = [i for i in range(1, number_of) if holding[i] < largest] or [i for i in range(1, number_of) if holding[i] < most]
        whole, remaining = sum([portions[i] for i in candidates]), surplus
        for i in candidates:
            addition = min(most - holding[i], max(1, remaining * portions[i] // whole), surplus)
            holding[i] = holding[i] + addition
            surplus = surplus - addition
    return np.array(holding)


def normal_values(rng, dims, scale, bound, cuts=(), held_as=jnp.bfloat16):
    gain = shard_levels(rng, dims, cuts, -0.22, 0.18) if cuts else 1.0
    entries = jax.random.normal(rng, dims, jnp.float32) * scale * gain
    return jnp.minimum(jnp.maximum(entries, -bound), bound).astype(held_as)


def setup_inputs(seed: int = 0) -> dict:
    arg_keys = jax.random.split(jax.random.key(seed), 9)
    queries = draw_queries(jax.random.fold_in(arg_keys[8], 71), 0)
    probe_groups_keys = jax.random.split(jax.random.fold_in(arg_keys[1], 1), QUERIES // Q_DEV)
    probe_groups_turns = jax.random.permutation(jax.random.fold_in(arg_keys[1], 3), QUERIES // Q_DEV)
    probe_groups = jax.vmap(lambda own, number: routed_block(jax.random.fold_in(arg_keys[1], 2), own, number, Q_DEV, N_CELL, 2, CAP, 2))(probe_groups_keys, probe_groups_turns).reshape((QUERIES, 2))
    probe_cells = draw_probe_cells(jax.random.fold_in(arg_keys[8], 71), 0)
    coarse = normal_values(arg_keys[3], (CELLS, DIM), 0.2, 1.1953125, ((0, 8), (1, 4)))
    codebooks = normal_values(arg_keys[4], (M, SD, K), 0.25, 1.5, ((0, 4),))
    codes = place_ends(jax.random.randint(arg_keys[5], (CELLS, M, ROWS), 0, K), jax.random.fold_in(arg_keys[5], 1), 0, K - 1).astype(jnp.int32)
    lengths = uneven_parts(arg_keys[6], CELLS, CELLS * ROWS // 2, ROWS, 2).astype(jnp.int32)
    payload = normal_values(arg_keys[7], (CELLS, ROWS, PW), 1.0, 6.0, ((0, 8), (1, 4)))
    return {"queries": queries, "probe_groups": probe_groups, "probe_cells": probe_cells, "coarse": coarse, "codebooks": codebooks, "codes": codes, "lengths": lengths, "payload": payload}


score_scale = 0.3
floor_score = -1.0e30


def decode_group(coarse_part, codebooks, codes_part):
    picked = jax.vmap(lambda book, index: book[:, index], in_axes=(0, 1))(codebooks, codes_part)
    recon = picked.reshape(DIM, CELL_DEV, ROWS).astype(jnp.float32)
    summed = recon + coarse_part.T.astype(jnp.float32)[:, :, None]
    return summed.astype(jnp.bfloat16).reshape(DIM, CELL_DEV * ROWS)


def reference(queries, probe_groups, probe_cells, coarse, codebooks, codes, lengths, payload):
    limit = N_CELL * CAP

    def one_group(group):
        start = group * CELL_DEV
        codes_part = lax.dynamic_slice_in_dim(codes, start, CELL_DEV, 0)
        coarse_part = lax.dynamic_slice_in_dim(coarse, start, CELL_DEV, 0)
        live_count = lax.dynamic_slice_in_dim(lengths, start, CELL_DEV, 0)
        table = lax.dynamic_slice_in_dim(payload, start, CELL_DEV, 0).reshape(CELL_DEV * ROWS, PW)
        decoded = decode_group(coarse_part, codebooks, codes_part)
        sq_norm = jnp.sum(jnp.square(decoded.astype(jnp.float32)), axis=0)
        hit = probe_groups == group
        routed = jnp.any(hit, axis=1)
        order = jnp.argsort(1 - routed.astype(jnp.int32), stable=True)[:limit].astype(jnp.int32)
        valid = routed[order]
        route = hit[order, 1].astype(jnp.int32)
        cells = probe_cells[order, route]
        probed = jnp.any(cells[:, :, None] == jnp.arange(CELL_DEV, dtype=jnp.int32)[None, None, :], axis=1)
        live = jnp.arange(ROWS, dtype=jnp.int32)[None, :] < live_count[:, None]
        keep = (probed[:, :, None] & live[None, :, :]).reshape(limit, CELL_DEV * ROWS)
        raw = jnp.dot(queries[order], decoded, preferred_element_type=jnp.float32)
        values = (raw - 0.5 * sq_norm[None, :]) * score_scale
        peak = jnp.max(jnp.where(keep, values, floor_score), axis=1)
        weights = jnp.where(keep, jnp.exp(values - peak[:, None]), 0.0).astype(jnp.bfloat16)
        mass = jnp.sum(weights.astype(jnp.float32), axis=1)
        part = jnp.dot(weights, table, preferred_element_type=jnp.float32)
        target = jnp.where(valid, order, QUERIES).astype(jnp.int32)
        return target, route, peak, mass, part

    target, route, peak, mass, part = lax.map(one_group, jnp.arange(N_CELL, dtype=jnp.int32))
    target = target.reshape(-1)
    route = route.reshape(-1)
    peaks = jnp.full((QUERIES, 2), floor_score, jnp.float32).at[target, route].set(peak.reshape(-1), mode="drop")
    masses = jnp.zeros((QUERIES, 2), jnp.float32).at[target, route].set(mass.reshape(-1), mode="drop")
    parts = jnp.zeros((QUERIES, 2, PW), jnp.float32).at[target, route].set(part.reshape(-1, PW), mode="drop")
    top = jnp.max(peaks, axis=1, keepdims=True)
    scale = jnp.exp(peaks - top)
    upper = jnp.sum(scale[:, :, None] * parts, axis=1)
    lower = jnp.sum(scale * masses, axis=1)
    return (upper / lower[:, None]).astype(jnp.bfloat16)
```

```python
import functools

import jax
import jax.numpy as jnp
from jax import lax
from jax.experimental import pallas as pl
from jax.experimental.pallas import tpu as pltpu
from jax.sharding import PartitionSpec as P

CAP = 64
LANES = 128
score_scale = 0.3
floor_score = -1e30
F32 = jnp.float32
BF16 = jnp.bfloat16


def iota(shape, dim):
    return lax.broadcasted_iota(jnp.int32, shape, dim)


def positions(meta_ref, groups):
    count = meta_ref.shape[1]
    padded = -(-groups // 8) * 8
    group_ids = iota((padded, count), 0)
    first = (meta_ref[0:1, :] == group_ids).astype(F32)
    second = (meta_ref[1:2, :] == group_ids).astype(F32)
    routed = first + second
    before = (iota((count, count), 0) < iota((count, count), 1)).astype(F32).astype(BF16)
    earlier = jnp.dot(routed.astype(BF16), before, preferred_element_type=F32)
    return first, second, routed, earlier


def pack_kernel(groups, half, meta_ref, rows_ref, buffer_ref, away_ref):
    count = meta_ref.shape[1]
    first, second, routed, earlier = positions(meta_ref, groups)
    spot = routed * (earlier + 1.0) - 1.0
    cell_ids = iota((LANES, count), 0)

    def named(start):
        marks = jnp.zeros((LANES, count), F32)
        for k in range(half):
            marks += (meta_ref[start + k : start + k + 1, :] == cell_ids).astype(F32)
        return marks

    named_first, named_second = named(2), named(2 + half)
    ranks = iota((CAP, count), 0).astype(F32)
    for g in range(groups):
        onehot = (ranks == spot[g : g + 1, :]).astype(F32).astype(BF16)
        buffer_ref[g * CAP : (g + 1) * CAP, :] = jnp.dot(
            onehot, rows_ref[...], preferred_element_type=F32
        ).astype(BF16)
        marks = first[g : g + 1, :] * named_first + second[g : g + 1, :] * named_second
        there = lax.dot_general(
            onehot, marks.astype(BF16), (((1,), (1,)), ((), ())), preferred_element_type=F32
        )
        away_ref[g * CAP : (g + 1) * CAP, :] = (1.0 - there).astype(BF16)


def score_kernel(
    row_local,
    codes_ref,
    books_ref,
    coarse_ref,
    lengths_ref,
    queries_ref,
    away_ref,
    values_ref,
    peak_ref,
    ids,
    vectors,
    squares,
    best,
):
    subs, rows = codes_ref.shape
    width = books_ref.shape[1]
    cells = coarse_ref.shape[0]
    blocks = rows // LANES
    ids[...] = codes_ref[...].astype(F32).astype(jnp.int32)
    offset = iota((cells, rows), 1) - iota((cells, rows), 0) * row_local
    inside = (offset >= 0) & (offset < row_local)
    spread = inside.astype(F32).astype(BF16)
    vectors[...] = lax.dot_general(
        coarse_ref[...], spread, (((0,), (0,)), ((), ())), preferred_element_type=F32
    ).astype(BF16)
    squares[...] = jnp.zeros_like(squares)

    @pl.loop(0, subs // 8)
    def _(group):
        for j in range(8):
            m = group * 8 + j
            book = books_ref[m].astype(F32)
            low, high = book[:, :LANES], book[:, LANES:]
            place = pl.ds(pl.multiple_of(m * width, width), width)
            for b in range(blocks):
                lanes = slice(b * LANES, (b + 1) * LANES)
                near = ids[pl.ds(pl.multiple_of(group * 8, 8), 8), lanes]
                code = jnp.broadcast_to(near[j : j + 1, :], (width, LANES))
                index = code & (LANES - 1)
                picked = jnp.where(
                    code < LANES,
                    jnp.take_along_axis(low, index, axis=1, mode="promise_in_bounds"),
                    jnp.take_along_axis(high, index, axis=1, mode="promise_in_bounds"),
                )
                summed = (picked + vectors[place, lanes].astype(F32)).astype(BF16)
                vectors[place, lanes] = summed
                back = summed.astype(F32)
                back = back * back
                squares[:, lanes] += back[:8] + back[8:]

    first_row = lax.axis_index("sub") * row_local
    live = jnp.sum(
        (inside & (offset + first_row < lengths_ref[...])).astype(F32), axis=0, keepdims=True
    )
    half_norm = 0.5 * jnp.sum(squares[...], axis=0, keepdims=True)
    squares[0:1, :] = jnp.where(live > 0.5, half_norm, -floor_score)
    step = 512 if rows % 512 == 0 else 256
    best[...] = jnp.full_like(best, 3.0 * floor_score)

    @pl.loop(0, rows // step)
    def _(n):
        lanes = pl.ds(pl.multiple_of(n * step, step), step)
        raw = jnp.dot(queries_ref[...], vectors[:, lanes], preferred_element_type=F32)
        shift = iota((LANES, step), 1) + n * step - iota((LANES, step), 0) * row_local
        far = jnp.where((shift >= 0) & (shift < row_local), floor_score, 0.0).astype(BF16)
        raw = raw + jnp.dot(away_ref[...], far, preferred_element_type=F32)
        values = (raw - squares[0:1, lanes]) * score_scale
        values_ref[:, lanes] = values
        top = best[...]
        for b in range(step // LANES):
            top = jnp.maximum(top, values[:, b * LANES : (b + 1) * LANES])
        best[...] = top

    peak_ref[...] = jnp.max(best[...], axis=1, keepdims=True)


def sum_kernel(values_ref, peak_ref, payload_ref, sums_ref):
    total = values_ref.shape[0]
    width = payload_ref.shape[1]
    block = 64

    @pl.loop(0, total // block)
    def _(n):
        place = pl.ds(pl.multiple_of(n * block, block), block)
        peak = peak_ref[place, :]
        weights = jnp.exp(values_ref[place, :] - peak).astype(BF16)
        mass = jnp.sum(weights.astype(F32), axis=1, keepdims=True)
        sums_ref[place, :width] = jnp.dot(weights, payload_ref[...], preferred_element_type=F32)
        lane = iota((block, LANES), 1)
        mine = (lax.axis_index("sub") == 0).astype(F32)
        sums_ref[place, width:] = jnp.where(
            lane == 0, mass, jnp.where(lane == 1, peak * mine, 0.0)
        )


def combine_kernel(groups, meta_ref, back_ref, pooled_ref):
    count = meta_ref.shape[1]
    total, wide = back_ref.shape
    width = wide - LANES
    first, second, _, earlier = positions(meta_ref, groups)

    def gathered(route, marks):
        spot = jnp.sum(marks * earlier, axis=0, keepdims=True).astype(jnp.int32)
        slot = meta_ref[route : route + 1, :] * CAP + spot
        onehot = (iota((total, count), 0) == slot).astype(F32).astype(BF16)

        def pick(part):
            return lax.dot_general(
                onehot, part, (((0,), (0,)), ((), ())), preferred_element_type=F32
            )

        sums = back_ref[...]
        out = jnp.zeros((count, wide), F32)
        for _ in range(3):
            piece = sums.astype(BF16)
            out = out + pick(piece)
            sums = sums - piece.astype(F32)
        return out[:, :width], out[:, width : width + 1], out[:, width + 1 : width + 2]

    part_0, mass_0, peak_0 = gathered(0, first)
    part_1, mass_1, peak_1 = gathered(1, second)
    top = jnp.maximum(peak_0, peak_1)
    scale_0, scale_1 = jnp.exp(peak_0 - top), jnp.exp(peak_1 - top)
    lower = scale_0 * mass_0 + scale_1 * mass_1
    pooled_ref[...] = ((scale_0 * part_0 + scale_1 * part_1) / lower).astype(BF16)


def call(kernel, outs, *args, scratch=()):
    spec = pl.BlockSpec(memory_space=pltpu.VMEM)
    return pl.pallas_call(
        kernel,
        out_shape=[jax.ShapeDtypeStruct(shape, dtype) for shape, dtype in outs],
        in_specs=[spec] * len(args),
        out_specs=[spec] * len(outs),
        scratch_shapes=list(scratch),
        compiler_params=pltpu.CompilerParams(vmem_limit_bytes=48 * 1024 * 1024),
    )(*args)


def local(queries, probe_groups, probe_cells, coarse, codebooks, codes, lengths, payload):
    groups, shares = lax.axis_size("cell"), lax.axis_size("sub")
    count, own_width = queries.shape
    half = probe_cells.shape[2]
    cells, own_subs, row_slots = codes.shape
    row_local = row_slots // shares
    rows = cells * row_local
    total = groups * CAP
    width = payload.shape[2]
    meta = jnp.concatenate([probe_groups, probe_cells.reshape(count, -1)], axis=1).T

    sent_codes = jnp.transpose(
        codes.astype(BF16).reshape(cells, own_subs, shares, row_local), (2, 1, 0, 3)
    ).reshape(shares, own_subs, rows)
    all_codes = lax.all_to_all(sent_codes, "sub", split_axis=0, concat_axis=0, tiled=True)
    all_codes = all_codes.reshape(shares * own_subs, rows)
    books = lax.all_gather(codebooks, "sub", axis=0, tiled=True)
    centers = lax.all_gather(coarse, "sub", axis=1, tiled=True)

    buffer, away = call(
        functools.partial(pack_kernel, groups, half),
        [((total, own_width), BF16), ((total, LANES), BF16)],
        meta,
        queries,
    )

    def swap(array):
        shape = array.shape
        return lax.all_to_all(
            array.reshape(groups, shape[0] // groups, shape[1]),
            "cell",
            split_axis=0,
            concat_axis=0,
            tiled=True,
        ).reshape(shape)

    buffer, away = swap(buffer), swap(away)
    full_rows = lax.all_gather(buffer, "sub", axis=1, tiled=True)

    values, peak = call(
        functools.partial(score_kernel, row_local),
        [((total, rows), F32), ((total, 1), F32)],
        all_codes,
        books,
        centers,
        lengths.reshape(cells, 1),
        full_rows,
        away,
        scratch=(
            pltpu.VMEM(all_codes.shape, jnp.int32),
            pltpu.VMEM((centers.shape[1], rows), BF16),
            pltpu.VMEM((8, rows), F32),
            pltpu.VMEM((total, LANES), F32),
        ),
    )
    peak = lax.pmax(peak, "sub")
    (sums,) = call(
        sum_kernel,
        [((total, width + LANES), F32)],
        values,
        peak,
        payload.reshape(rows, width),
    )
    wide = width + LANES
    shared = lax.psum_scatter(
        sums.reshape(groups, CAP, wide), "sub", scatter_dimension=1, tiled=True
    )
    back = lax.all_to_all(shared, "cell", split_axis=0, concat_axis=0, tiled=True)
    back = lax.all_gather(back, "sub", axis=1, tiled=True).reshape(total, wide)
    (pooled,) = call(
        functools.partial(combine_kernel, groups), [((count, width), BF16)], meta, back
    )
    return pooled


def solution(mesh):
    placed = (
        P("cell", "sub"),
        P("cell", None),
        P("cell", None, None),
        P("cell", "sub"),
        P("sub", None, None),
        P("cell", "sub", None),
        P("cell"),
        P("cell", "sub", None),
    )
    return jax.shard_map(
        local, mesh=mesh, in_specs=placed, out_specs=P("cell", None), check_vma=False
    )
```

```python
import functools

import jax
import jax.numpy as jnp
from jax import lax
from jax.experimental import pallas as pl
from jax.experimental.pallas import tpu as pltpu
from jax.sharding import PartitionSpec as P

CAP = 64
LANES = 128
score_scale = 0.3
floor_score = -1e30
F32 = jnp.float32
BF16 = jnp.bfloat16


def iota(shape, dim):
    return lax.broadcasted_iota(jnp.int32, shape, dim)


def positions(meta_ref, groups):
    count = meta_ref.shape[1]
    padded = -(-groups // 8) * 8
    group_ids = iota((padded, count), 0)
    first = (meta_ref[0:1, :] == group_ids).astype(F32)
    second = (meta_ref[1:2, :] == group_ids).astype(F32)
    routed = first + second
    before = (iota((count, count), 0) < iota((count, count), 1)).astype(F32).astype(BF16)
    earlier = jnp.dot(routed.astype(BF16), before, preferred_element_type=F32)
    return first, second, routed, earlier


def pack_kernel(groups, half, meta_ref, rows_ref, buffer_ref, away_ref):
    count = meta_ref.shape[1]
    first, second, routed, earlier = positions(meta_ref, groups)
    spot = routed * (earlier + 1.0) - 1.0
    cell_ids = iota((LANES, count), 0)

    def named(start):
        marks = jnp.zeros((LANES, count), F32)
        for k in range(half):
            marks += (meta_ref[start + k : start + k + 1, :] == cell_ids).astype(F32)
        return marks

    named_first, named_second = named(2), named(2 + half)
    ranks = iota((CAP, count), 0).astype(F32)
    for g in range(groups):
        onehot = (ranks == spot[g : g + 1, :]).astype(F32).astype(BF16)
        buffer_ref[g] = jnp.dot(
            onehot, rows_ref[...], preferred_element_type=F32
        ).astype(BF16)
        marks = first[g : g + 1, :] * named_first + second[g : g + 1, :] * named_second
        there = lax.dot_general(
            onehot, marks.astype(BF16), (((1,), (1,)), ((), ())), preferred_element_type=F32
        )
        away_ref[g] = (1.0 - there).astype(BF16)


def decode_share(subs, width, blocks, codes_ref, books_ref, base, ids, vectors, squares):
    near = min(8, subs)
    ids[...] = codes_ref[...].astype(F32).astype(jnp.int32)

    def some(start):
        @pl.loop(0, blocks // 2)
        def _(pair):
            for u in range(2):
                lanes = pl.ds(pl.multiple_of(pair * (2 * LANES) + u * LANES, LANES), LANES)
                held = ids[pl.ds(start, near), lanes]
                total = jnp.zeros((8, LANES), F32)
                for j in range(near):
                    book = books_ref[start + j].astype(F32)
                    code = jnp.broadcast_to(held[j : j + 1, :], (width, LANES))
                    index = code & (LANES - 1)
                    picked = jnp.where(
                        code < LANES,
                        jnp.take_along_axis(book[:, :LANES], index, axis=1, mode="promise_in_bounds"),
                        jnp.take_along_axis(book[:, LANES:], index, axis=1, mode="promise_in_bounds"),
                    )
                    place = pl.ds(pl.multiple_of(base + (start + j) * width, width), width)
                    summed = (picked + vectors[place, lanes].astype(F32)).astype(BF16)
                    vectors[place, lanes] = summed
                    back = summed.astype(F32)
                    back = back * back
                    total += back[:8] + back[8:]
                squares[:, lanes] += total

    if subs == near:
        some(0)
    else:

        @pl.loop(0, subs // near)
        def _(group):
            some(pl.multiple_of(group * near, near))


def whole_kernel(
    groups,
    shares,
    half,
    row_local,
    fold,
    meta_ref,
    rows_ref,
    codes_ref,
    books_ref,
    coarse_ref,
    lengths_ref,
    payload_ref,
    pooled_ref,
    buffer,
    away_out,
    queries,
    away,
    codes_in,
    books_in,
    coarse_in,
    ids,
    vectors,
    squares,
    best,
    values,
    peak_row,
    part,
    masses,
    mass_row,
    share_out,
    share_in,
    back_out,
    back_in,
    stat_out,
    stat_in,
    columns,
    send_sem,
    recv_sem,
):
    me_cell, me_sub = lax.axis_index("cell"), lax.axis_index("sub")
    count = meta_ref.shape[1]
    subs, rows = ids.shape
    book_width = books_ref.shape[1]
    cells, own_width = coarse_ref.shape
    total = groups * CAP
    width = payload_ref.shape[1]
    own_columns = width // shares
    short = CAP // fold
    blocks = rows // LANES
    step = 512 if rows % 512 == 0 else 256
    used = [0]

    def device(cell_off, sub_off):
        return (lax.rem(me_cell + cell_off, groups), lax.rem(me_sub + sub_off, shares))

    def send(src, dst, cell_off, sub_off):
        i = used[0]
        used[0] += 1
        copy = pltpu.make_async_remote_copy(
            src_ref=src,
            dst_ref=dst,
            send_sem=send_sem.at[i],
            recv_sem=recv_sem.at[i],
            device_id=device(cell_off, sub_off),
            device_id_type=pl.DeviceIdType.MESH,
        )
        copy.start()
        return copy

    barrier = pltpu.get_barrier_semaphore()
    for off in range(1, groups):
        pl.semaphore_signal(
            barrier, inc=1, device_id=device(off, 0), device_id_type=pl.DeviceIdType.MESH
        )
    for off in range(1, shares):
        pl.semaphore_signal(
            barrier, inc=1, device_id=device(0, off), device_id_type=pl.DeviceIdType.MESH
        )
    pl.semaphore_wait(barrier, groups + shares - 2)

    everything = []
    lists = [None]
    for off in range(1, shares):
        target = lax.rem(me_sub + off, shares)
        lists.append(
            [
                send(codes_ref.at[target], codes_in.at[off - 1], 0, off),
                send(books_ref, books_in.at[off - 1], 0, off),
                send(coarse_ref, coarse_in.at[off - 1], 0, off),
            ]
        )
        everything += lists[-1]

    pack_kernel(groups, half, meta_ref, rows_ref, buffer, away_out)
    routed = [None]
    for off in range(1, groups):
        target = lax.rem(me_cell + off, groups)
        routed.append(
            [
                send(buffer.at[target], queries.at[0, me_cell], off, 0),
                send(away_out.at[target], away.at[me_cell], off, 0),
            ]
        )
        everything += routed[-1]
    queries[0, me_cell] = buffer[me_cell]
    away[me_cell] = away_out[me_cell]
    spread_out = []

    def forward(off):
        if off:
            for copy in routed[off]:
                copy.wait_recv()
        source = lax.rem(me_cell + groups - off, groups)
        for sub_off in range(1, shares):
            spread_out.append(
                send(queries.at[0, source], queries.at[sub_off, source], 0, sub_off)
            )

    forward(0)
    squares[...] = jnp.zeros_like(squares)
    passed = 1
    for k in range(shares):
        if k:
            for copy in lists[k]:
                copy.wait_recv()
        centers = coarse_in.at[k - 1] if k else coarse_ref

        @pl.loop(0, rows // step)
        def _(n):
            lanes = pl.ds(pl.multiple_of(n * step, step), step)
            shift = iota((cells, step), 1) + n * step - iota((cells, step), 0) * row_local
            inside = ((shift >= 0) & (shift < row_local)).astype(F32).astype(BF16)
            vectors[k * own_width : (k + 1) * own_width, lanes] = lax.dot_general(
                centers[...], inside, (((0,), (0,)), ((), ())), preferred_element_type=F32
            ).astype(BF16)

        decode_share(
            subs,
            book_width,
            blocks,
            codes_in.at[k - 1] if k else codes_ref.at[me_sub],
            books_in.at[k - 1] if k else books_ref,
            k * own_width,
            ids,
            vectors,
            squares,
        )
        until = min(groups, 1 + -(-(groups - 1) * (k + 1) // min(shares, 2)))
        for off in range(passed, until):
            forward(off)
        passed = max(passed, until)
    everything += spread_out

    offset = iota((cells, rows), 1) - iota((cells, rows), 0) * row_local
    inside = (offset >= 0) & (offset < row_local)
    live = jnp.sum(
        (inside & (offset + me_sub * row_local < lengths_ref[...])).astype(F32),
        axis=0,
        keepdims=True,
    )
    half_norm = 0.5 * jnp.sum(squares[...], axis=0, keepdims=True)
    squares[0:1, :] = jnp.where(live > 0.5, half_norm, -floor_score)
    best[...] = jnp.full_like(best, 3.0 * floor_score)
    for copy in spread_out:
        copy.wait_recv()

    @pl.loop(0, rows // step)
    def _(n):
        lanes = pl.ds(pl.multiple_of(n * step, step), step)
        shift = iota((LANES, step), 1) + n * step - iota((LANES, step), 0) * row_local
        far = jnp.where((shift >= 0) & (shift < row_local), floor_score, 0.0).astype(BF16)
        raw = jnp.dot(away[...].reshape(total, LANES), far, preferred_element_type=F32)
        for k in range(shares):
            raw = raw + jnp.dot(
                queries[k].reshape(total, own_width),
                vectors[k * own_width : (k + 1) * own_width, lanes],
                preferred_element_type=F32,
            )
        scores = (raw - squares[0:1, lanes]) * score_scale
        values[:, lanes] = scores
        top = best[...]
        for b in range(step // LANES):
            top = jnp.maximum(top, scores[:, b * LANES : (b + 1) * LANES])
        best[...] = top

    peak_row[0] = jnp.broadcast_to(
        jnp.max(jnp.transpose(best[...]), axis=0, keepdims=True), (8, total)
    )
    tops = [send(peak_row.at[0], peak_row.at[off], 0, off) for off in range(1, shares)]
    everything += tops
    for copy in tops:
        copy.wait_recv()
    peak = jnp.max(peak_row[...], axis=0)
    best[...] = jnp.transpose(jnp.broadcast_to(peak[0:1], (LANES, total)))
    part[...] = jnp.zeros_like(part)
    masses[...] = jnp.zeros_like(masses)

    @pl.loop(0, rows // step)
    def _(n):
        lanes = pl.ds(pl.multiple_of(n * step, step), step)
        mass = masses[...]
        pieces = []
        for b in range(step // LANES):
            inner = pl.ds(pl.multiple_of(n * step + b * LANES, LANES), LANES)
            piece = jnp.exp(values[:, inner] - best[...]).astype(BF16)
            mass = mass + piece.astype(F32)
            pieces.append(piece)
        masses[...] = mass
        part[...] += jnp.dot(
            jnp.concatenate(pieces, axis=1), payload_ref[lanes, :], preferred_element_type=F32
        )

    mass_row[0] = jnp.broadcast_to(
        jnp.sum(jnp.transpose(masses[...]), axis=0, keepdims=True), (8, total)
    )
    sums = part[...].reshape(groups, CAP, width)
    for t in range(shares):
        own = slice(t * own_columns, (t + 1) * own_columns)
        share_out[t] = jnp.concatenate(
            [sums[:, b * short : (b + 1) * short, own] for b in range(fold)], axis=2
        ).astype(share_out.dtype)
    shared = []
    for off in range(1, shares):
        target = lax.rem(me_sub + off, shares)
        shared.append(send(share_out.at[target], share_in.at[off - 1], 0, off))
        shared.append(send(mass_row.at[0], mass_row.at[off], 0, off))
    everything += shared
    for copy in shared:
        copy.wait_recv()
    share = share_out[me_sub].astype(F32)
    for off in range(1, shares):
        share = share + share_in[off - 1].astype(F32)
    back_out[...] = share
    mass_all = mass_row[0]
    for off in range(1, shares):
        mass_all = mass_all + mass_row[off]
    stats = jnp.where(iota((8, total), 0) == 0, mass_all, peak)
    for g in range(groups):
        mine = stats[:, g * CAP : (g + 1) * CAP]
        stat_out[g] = jnp.concatenate([mine, jnp.zeros((8, LANES - CAP), F32)], axis=1)
    returned = []
    for off in range(1, groups):
        target = lax.rem(me_cell + off, groups)
        returned.append(send(back_out.at[target], back_in.at[me_cell], off, 0))
        returned.append(send(stat_out.at[target], stat_in.at[me_cell], off, 0))
    everything += returned
    back_in[me_cell] = back_out[me_cell]
    stat_in[me_cell] = stat_out[me_cell]

    first, second, _, earlier = positions(meta_ref, groups)
    marks = []
    for route, named in ((0, first), (1, second)):
        spot = jnp.sum(
            named * earlier, axis=0, keepdims=True
        ).astype(jnp.int32)
        slot = meta_ref[route : route + 1, :] * CAP + spot
        marks.append((iota((total, count), 0) == slot).astype(F32).astype(BF16))
    for copy in returned:
        copy.wait_recv()

    def pick(array, mark, dim):
        out = 0.0
        for _ in range(3):
            piece = array.astype(BF16)
            out = out + lax.dot_general(
                piece, mark, (((dim,), (0,)), ((), ())), preferred_element_type=F32
            )
            array = array - piece.astype(F32)
        return out

    held = back_in[...]
    table = jnp.concatenate(
        [held[:, :, b * own_columns : (b + 1) * own_columns] for b in range(fold)], axis=1
    ).reshape(total, own_columns)
    stat_row = jnp.concatenate([stat_in[g][:, :CAP] for g in range(groups)], axis=1)
    stat_0, stat_1 = pick(stat_row, marks[0], 1), pick(stat_row, marks[1], 1)
    top = jnp.maximum(stat_0[1:2], stat_1[1:2])
    scale_0, scale_1 = jnp.exp(stat_0[1:2] - top), jnp.exp(stat_1[1:2] - top)
    lower = scale_0 * stat_0[0:1] + scale_1 * stat_1[0:1]
    upper = scale_0 * pick(table, marks[0], 0) + scale_1 * pick(table, marks[1], 0)
    columns[me_sub] = (upper / lower).astype(BF16)
    gathered = [
        send(columns.at[me_sub], columns.at[me_sub], 0, off) for off in range(1, shares)
    ]
    everything += gathered
    for copy in gathered:
        copy.wait_recv()
    pooled_ref[...] = jnp.transpose(
        columns[...].astype(F32).reshape(width, count)
    ).astype(BF16)
    for copy in everything:
        copy.wait_send()


def local(queries, probe_groups, probe_cells, coarse, codebooks, codes, lengths, payload):
    groups, shares = lax.axis_size("cell"), lax.axis_size("sub")
    count, own_width = queries.shape
    half = probe_cells.shape[2]
    cells, own_subs, row_slots = codes.shape
    row_local = row_slots // shares
    rows = cells * row_local
    total = groups * CAP
    width = payload.shape[2]
    fold = LANES // (width // shares)
    short = CAP // fold
    meta = jnp.concatenate([probe_groups, probe_cells.reshape(count, -1)], axis=1).T
    sent_codes = jnp.transpose(
        codes.astype(BF16).reshape(cells, own_subs, shares, row_local), (2, 1, 0, 3)
    ).reshape(shares, own_subs, rows)
    copies = 3 * (shares - 1) + 4 * (groups - 1) + (groups + 4) * (shares - 1)
    spec = pl.BlockSpec(memory_space=pltpu.VMEM)
    return pl.pallas_call(
        functools.partial(whole_kernel, groups, shares, half, row_local, fold),
        out_shape=jax.ShapeDtypeStruct((count, width), BF16),
        in_specs=[spec] * 7,
        out_specs=spec,
        scratch_shapes=[
            pltpu.VMEM((groups, CAP, own_width), BF16),
            pltpu.VMEM((groups, CAP, LANES), BF16),
            pltpu.VMEM((shares, groups, CAP, own_width), BF16),
            pltpu.VMEM((groups, CAP, LANES), BF16),
            pltpu.VMEM((shares - 1, own_subs, rows), BF16),
            pltpu.VMEM((shares - 1,) + codebooks.shape, BF16),
            pltpu.VMEM((shares - 1,) + coarse.shape, BF16),
            pltpu.VMEM((own_subs, rows), jnp.int32),
            pltpu.VMEM((shares * own_width, rows), BF16),
            pltpu.VMEM((8, rows), F32),
            pltpu.VMEM((total, LANES), F32),
            pltpu.VMEM((total, rows), F32),
            pltpu.VMEM((shares, 8, total), F32),
            pltpu.VMEM((total, width), F32),
            pltpu.VMEM((total, LANES), F32),
            pltpu.VMEM((shares, 8, total), F32),
            pltpu.VMEM((shares, groups, short, LANES), F32),
            pltpu.VMEM((shares - 1, groups, short, LANES), F32),
            pltpu.VMEM((groups, short, LANES), F32),
            pltpu.VMEM((groups, short, LANES), F32),
            pltpu.VMEM((groups, 8, LANES), F32),
            pltpu.VMEM((groups, 8, LANES), F32),
            pltpu.VMEM((shares, width // shares, count), BF16),
            pltpu.SemaphoreType.DMA((copies,)),
            pltpu.SemaphoreType.DMA((copies,)),
        ],
        compiler_params=pltpu.CompilerParams(
            collective_id=0, has_side_effects=True, vmem_limit_bytes=56 * 1024 * 1024
        ),
    )(meta, queries, sent_codes, codebooks, coarse, lengths.reshape(cells, 1), payload.reshape(rows, width))


def solution(mesh):
    placed = (
        P("cell", "sub"),
        P("cell", None),
        P("cell", None, None),
        P("cell", "sub"),
        P("sub", None, None),
        P("cell", "sub", None),
        P("cell"),
        P("cell", "sub", None),
    )
    return jax.shard_map(
        local, mesh=mesh, in_specs=placed, out_specs=P("cell", None), check_vma=False
    )
```

```python
import functools
import math

import jax
import jax.numpy as jnp
from jax import lax
from jax.experimental import pallas as pl
from jax.experimental.pallas import tpu as pltpu
from jax.sharding import PartitionSpec as P

CAP = 64
HALVES = 2
LANES = 128
score_scale = 0.3
floor_score = -1e30
F32 = jnp.float32
BF16 = jnp.bfloat16


def iota(shape, dim):
    return lax.broadcasted_iota(jnp.int32, shape, dim)


def positions(meta_ref, groups):
    count = meta_ref.shape[1]
    padded = -(-groups // 8) * 8
    group_ids = iota((padded, count), 0)
    first = (meta_ref[0:1, :] == group_ids).astype(F32)
    second = (meta_ref[1:2, :] == group_ids).astype(F32)
    routed = first + second
    before = (iota((count, count), 0) < iota((count, count), 1)).astype(F32).astype(BF16)
    earlier = jnp.dot(routed.astype(BF16), before, preferred_element_type=F32)
    return first, second, routed, earlier


def pack_kernel(groups, half, meta_ref, rows_ref, buffer_ref, away_ref):
    count = meta_ref.shape[1]
    first, second, routed, earlier = positions(meta_ref, groups)
    spot = routed * (earlier + 1.0) - 1.0
    cell_ids = iota((LANES, count), 0)

    def named(start):
        marks = jnp.zeros((LANES, count), F32)
        for k in range(half):
            marks += (meta_ref[start + k : start + k + 1, :] == cell_ids).astype(F32)
        return marks

    named_first, named_second = named(2), named(2 + half)
    ranks = iota((CAP, count), 0).astype(F32)
    for g in range(groups):
        onehot = (ranks == spot[g : g + 1, :]).astype(F32).astype(BF16)
        buffer_ref[g] = jnp.dot(
            onehot, rows_ref[...], preferred_element_type=F32
        ).astype(BF16)
        marks = first[g : g + 1, :] * named_first + second[g : g + 1, :] * named_second
        there = lax.dot_general(
            onehot, marks.astype(BF16), (((1,), (1,)), ((), ())), preferred_element_type=F32
        )
        away_ref[g] = (1.0 - there).astype(BF16)


def decode_share(subs, width, blocks, codes_ref, books_ref, base, ids, vectors, squares):
    near = min(8, subs)
    ids[...] = codes_ref[...].astype(F32).astype(jnp.int32)

    def some(start):
        @pl.loop(0, blocks // 2)
        def _(pair):
            for u in range(2):
                lanes = pl.ds(pl.multiple_of(pair * (2 * LANES) + u * LANES, LANES), LANES)
                held = ids[pl.ds(start, near), lanes]
                total = jnp.zeros((8, LANES), F32)
                for j in range(near):
                    book = books_ref[start + j].astype(F32)
                    code = jnp.broadcast_to(held[j : j + 1, :], (width, LANES))
                    index = code & (LANES - 1)
                    picked = jnp.where(
                        code < LANES,
                        jnp.take_along_axis(book[:, :LANES], index, axis=1, mode="promise_in_bounds"),
                        jnp.take_along_axis(book[:, LANES:], index, axis=1, mode="promise_in_bounds"),
                    )
                    place = pl.ds(pl.multiple_of(base + (start + j) * width, width), width)
                    summed = (picked + vectors[place, lanes].astype(F32)).astype(BF16)
                    vectors[place, lanes] = summed
                    back = summed.astype(F32)
                    back = back * back
                    total += back[:8] + back[8:]
                squares[:, lanes] += total

    if subs == near:
        some(0)
    else:

        @pl.loop(0, subs // near)
        def _(group):
            some(pl.multiple_of(group * near, near))


def whole_kernel(
    groups,
    shares,
    half,
    row_local,
    fold,
    meta_ref,
    rows_ref,
    raw_codes_ref,
    books_ref,
    coarse_ref,
    lengths_ref,
    payload_ref,
    pooled_ref,
    codes_ref,
    buffer,
    away_out,
    queries,
    away,
    codes_in,
    books_in,
    coarse_in,
    ids,
    vectors,
    squares,
    best,
    values,
    peak_row,
    part,
    masses,
    mass_row,
    share_out,
    share_in,
    back_out,
    back_in,
    stat_out,
    stat_in,
    columns,
    send_sem,
    recv_sem,
):
    me_cell, me_sub = lax.axis_index("cell"), lax.axis_index("sub")
    count = meta_ref.shape[1]
    subs, rows = ids.shape
    book_width = books_ref.shape[1]
    cells, own_width = coarse_ref.shape
    total = groups * CAP
    width = payload_ref.shape[1]
    own_columns = width // shares
    short = CAP // fold // HALVES
    blocks = rows // LANES
    step = 512 if rows % 512 == 0 else 256
    used = [0]

    def device(cell_off, sub_off):
        return (lax.rem(me_cell + cell_off, groups), lax.rem(me_sub + sub_off, shares))

    def send(src, dst, cell_off, sub_off):
        i = used[0]
        used[0] += 1
        copy = pltpu.make_async_remote_copy(
            src_ref=src,
            dst_ref=dst,
            send_sem=send_sem.at[i],
            recv_sem=recv_sem.at[i],
            device_id=device(cell_off, sub_off),
            device_id_type=pl.DeviceIdType.MESH,
        )
        copy.start()
        return copy

    barrier = pltpu.get_barrier_semaphore()
    for off in range(1, groups):
        pl.semaphore_signal(
            barrier, inc=1, device_id=device(off, 0), device_id_type=pl.DeviceIdType.MESH
        )
    for off in range(1, shares):
        pl.semaphore_signal(
            barrier, inc=1, device_id=device(0, off), device_id_type=pl.DeviceIdType.MESH
        )
    several = LANES // math.gcd(row_local, LANES)
    for t in range(shares):
        for start in range(0, cells, several):
            codes_ref[t, :, start * row_local : (start + several) * row_local] = jnp.concatenate(
                [
                    raw_codes_ref[c, :, t * row_local : (t + 1) * row_local]
                    for c in range(start, start + several)
                ],
                axis=1,
            ).astype(F32).astype(BF16)
    pack_kernel(groups, half, meta_ref, rows_ref, buffer, away_out)
    pl.semaphore_wait(barrier, groups + shares - 2)

    everything = []
    routed = [None]
    for off in range(1, groups):
        target = lax.rem(me_cell + off, groups)
        routed.append(
            [
                send(buffer.at[target], queries.at[0, me_cell], off, 0),
                send(away_out.at[target], away.at[me_cell], off, 0),
            ]
        )
        everything += routed[-1]
    lists = [None]
    for off in range(1, shares):
        target = lax.rem(me_sub + off, shares)
        lists.append(
            [
                send(codes_ref.at[target], codes_in.at[off - 1], 0, off),
                send(books_ref, books_in.at[off - 1], 0, off),
                send(coarse_ref, coarse_in.at[off - 1], 0, off),
            ]
        )
        everything += lists[-1]

    queries[0, me_cell] = buffer[me_cell]
    away[me_cell] = away_out[me_cell]
    spread_out = []

    def forward(off):
        if off:
            for copy in routed[off]:
                copy.wait_recv()
        source = lax.rem(me_cell + groups - off, groups)
        for sub_off in range(1, shares):
            spread_out.append(
                send(queries.at[0, source], queries.at[sub_off, source], 0, sub_off)
            )

    forward(0)
    squares[...] = jnp.zeros_like(squares)
    passed = 1
    for k in range(shares):
        if k:
            for copy in lists[k]:
                copy.wait_recv()
        centers = coarse_in.at[k - 1] if k else coarse_ref

        @pl.loop(0, rows // step)
        def _(n):
            lanes = pl.ds(pl.multiple_of(n * step, step), step)
            shift = iota((cells, step), 1) + n * step - iota((cells, step), 0) * row_local
            inside = ((shift >= 0) & (shift < row_local)).astype(F32).astype(BF16)
            vectors[k * own_width : (k + 1) * own_width, lanes] = lax.dot_general(
                centers[...], inside, (((0,), (0,)), ((), ())), preferred_element_type=F32
            ).astype(BF16)

        decode_share(
            subs,
            book_width,
            blocks,
            codes_in.at[k - 1] if k else codes_ref.at[me_sub],
            books_in.at[k - 1] if k else books_ref,
            k * own_width,
            ids,
            vectors,
            squares,
        )
        until = min(groups, 1 + -(-(groups - 1) * (k + 1) // min(shares, 2)))
        for off in range(passed, until):
            forward(off)
        passed = max(passed, until)
    everything += spread_out

    offset = iota((cells, rows), 1) - iota((cells, rows), 0) * row_local
    inside = (offset >= 0) & (offset < row_local)
    reach = jnp.zeros((cells, 1), jnp.int32)
    for c in range(cells):
        reach = jnp.where(iota((cells, 1), 0) == c, lengths_ref[c], reach)
    live = jnp.sum(
        (inside & (offset + me_sub * row_local < reach)).astype(F32),
        axis=0,
        keepdims=True,
    )
    half_norm = 0.5 * jnp.sum(squares[...], axis=0, keepdims=True)
    squares[0:1, :] = jnp.where(live > 0.5, half_norm, -floor_score)
    for copy in spread_out:
        copy.wait_recv()
    part_cap = CAP // HALVES
    part_total = total // HALVES

    def score(h):
        some = slice(h * part_cap, (h + 1) * part_cap)
        best[h] = jnp.full(best.shape[1:], 3.0 * floor_score, F32)

        @pl.loop(0, rows // step)
        def _(n):
            lanes = pl.ds(pl.multiple_of(n * step, step), step)
            shift = iota((LANES, step), 1) + n * step - iota((LANES, step), 0) * row_local
            far = jnp.where((shift >= 0) & (shift < row_local), floor_score, 0.0).astype(BF16)
            raw = jnp.dot(
                away[:, some].reshape(part_total, LANES), far, preferred_element_type=F32
            )
            for k in range(shares):
                raw = raw + jnp.dot(
                    queries[k, :, some].reshape(part_total, own_width),
                    vectors[k * own_width : (k + 1) * own_width, lanes],
                    preferred_element_type=F32,
                )
            scores = (raw - squares[0:1, lanes]) * score_scale
            values[h, :, lanes] = scores
            top = best[h]
            for b in range(step // LANES):
                top = jnp.maximum(top, scores[:, b * LANES : (b + 1) * LANES])
            best[h] = top

        peak_row[h, 0] = jnp.broadcast_to(
            jnp.max(jnp.transpose(best[h]), axis=0, keepdims=True), (8, part_total)
        )
        return [
            send(peak_row.at[h, 0], peak_row.at[h, off], 0, off) for off in range(1, shares)
        ]

    def pool(h, tops):
        for copy in tops:
            copy.wait_recv()
        peak = jnp.max(peak_row[h], axis=0)
        best[h] = jnp.transpose(jnp.broadcast_to(peak[0:1], (LANES, part_total)))
        part[...] = jnp.zeros_like(part)
        masses[...] = jnp.zeros_like(masses)

        @pl.loop(0, rows // step)
        def _(n):
            lanes = pl.ds(pl.multiple_of(n * step, step), step)
            mass = masses[...]
            pieces = []
            for b in range(step // LANES):
                inner = pl.ds(pl.multiple_of(n * step + b * LANES, LANES), LANES)
                piece = jnp.exp(values[h, :, inner] - best[h]).astype(BF16)
                mass = mass + piece.astype(F32)
                pieces.append(piece)
            masses[...] = mass
            part[...] += jnp.dot(
                jnp.concatenate(pieces, axis=1),
                payload_ref[lanes, :],
                preferred_element_type=F32,
            )

        mass_row[h, 0] = jnp.broadcast_to(
            jnp.sum(jnp.transpose(masses[...]), axis=0, keepdims=True), (8, part_total)
        )
        sums = part[...].reshape(groups, part_cap, width)
        for t in range(shares):
            own = slice(t * own_columns, (t + 1) * own_columns)
            share_out[h, t] = jnp.concatenate(
                [sums[:, b * short : (b + 1) * short, own] for b in range(fold)], axis=2
            ).astype(share_out.dtype)
        shared = []
        for off in range(1, shares):
            target = lax.rem(me_sub + off, shares)
            shared.append(send(share_out.at[h, target], share_in.at[h, off - 1], 0, off))
            shared.append(send(mass_row.at[h, 0], mass_row.at[h, off], 0, off))
        return shared, peak

    def give_back(h, shared, peak):
        for copy in shared:
            copy.wait_recv()
        share = share_out[h, me_sub].astype(F32)
        for off in range(1, shares):
            share = share + share_in[h, off - 1].astype(F32)
        back_out[h] = share
        sent = []
        for off in range(1, groups):
            target = lax.rem(me_cell + off, groups)
            sent.append(send(back_out.at[h, target], back_in.at[h, me_cell], off, 0))
        back_in[h, me_cell] = back_out[h, me_cell]
        mass_all = mass_row[h, 0]
        for off in range(1, shares):
            mass_all = mass_all + mass_row[h, off]
        return sent, jnp.where(iota((8, part_total), 0) == 0, mass_all, peak)

    tops = [score(h) for h in range(HALVES)]
    pooled = [pool(h, tops[h]) for h in range(HALVES)]
    given = [give_back(h, *pooled[h]) for h in range(HALVES)]
    returned = []
    for h in range(HALVES):
        everything += tops[h] + pooled[h][0] + given[h][0]
        returned += given[h][0]
    for g in range(groups):
        mine = [stats[:, g * part_cap : (g + 1) * part_cap] for _, stats in given]
        stat_out[g] = jnp.concatenate(mine + [jnp.zeros((8, LANES - CAP), F32)], axis=1)
    stat_sent = []
    for off in range(1, groups):
        target = lax.rem(me_cell + off, groups)
        stat_sent.append(send(stat_out.at[target], stat_in.at[me_cell], off, 0))
    everything += stat_sent
    returned += stat_sent
    stat_in[me_cell] = stat_out[me_cell]

    first, second, _, earlier = positions(meta_ref, groups)
    marks = []
    for route, named in ((0, first), (1, second)):
        spot = jnp.sum(
            named * earlier, axis=0, keepdims=True
        ).astype(jnp.int32)
        slot = meta_ref[route : route + 1, :] * CAP + spot
        marks.append((iota((total, count), 0) == slot).astype(F32).astype(BF16))
    for copy in returned:
        copy.wait_recv()

    def pick(array, mark, dim):
        out = 0.0
        for _ in range(3):
            piece = array.astype(BF16)
            out = out + lax.dot_general(
                piece, mark, (((dim,), (0,)), ((), ())), preferred_element_type=F32
            )
            array = array - piece.astype(F32)
        return out

    table = jnp.concatenate(
        [
            back_in[h][:, :, b * own_columns : (b + 1) * own_columns]
            for h in range(HALVES)
            for b in range(fold)
        ],
        axis=1,
    ).reshape(total, own_columns)
    stat_row = jnp.concatenate([stat_in[g][:, :CAP] for g in range(groups)], axis=1)
    stat_0, stat_1 = pick(stat_row, marks[0], 1), pick(stat_row, marks[1], 1)
    top = jnp.maximum(stat_0[1:2], stat_1[1:2])
    scale_0, scale_1 = jnp.exp(stat_0[1:2] - top), jnp.exp(stat_1[1:2] - top)
    lower = scale_0 * stat_0[0:1] + scale_1 * stat_1[0:1]
    upper = scale_0 * pick(table, marks[0], 0) + scale_1 * pick(table, marks[1], 0)
    columns[me_sub] = (upper / lower).astype(BF16)
    gathered = [
        send(columns.at[me_sub], columns.at[me_sub], 0, off) for off in range(1, shares)
    ]
    everything += gathered
    for copy in gathered:
        copy.wait_recv()
    pooled_ref[...] = columns[...].reshape(width, count)
    for copy in everything:
        copy.wait_send()


def local(queries, probe_groups, probe_cells, coarse, codebooks, codes, lengths, payload):
    groups, shares = lax.axis_size("cell"), lax.axis_size("sub")
    count, own_width = queries.shape
    half = probe_cells.shape[2]
    cells, own_subs, row_slots = codes.shape
    row_local = row_slots // shares
    rows = cells * row_local
    total = groups * CAP
    width = payload.shape[2]
    fold = LANES // (width // shares)
    short = CAP // fold // HALVES
    meta = jnp.concatenate([probe_groups, probe_cells.reshape(count, -1)], axis=1).T
    copies = (3 + HALVES) * (groups - 1) + (groups + 4 + 3 * HALVES) * (shares - 1)
    spec = pl.BlockSpec(memory_space=pltpu.VMEM)
    pooled = pl.pallas_call(
        functools.partial(whole_kernel, groups, shares, half, row_local, fold),
        out_shape=jax.ShapeDtypeStruct((width, count), BF16),
        in_specs=[spec] * 5 + [pl.BlockSpec(memory_space=pltpu.SMEM), spec],
        out_specs=spec,
        scratch_shapes=[
            pltpu.VMEM((shares, own_subs, rows), BF16),
            pltpu.VMEM((groups, CAP, own_width), BF16),
            pltpu.VMEM((groups, CAP, LANES), BF16),
            pltpu.VMEM((shares, groups, CAP, own_width), BF16),
            pltpu.VMEM((groups, CAP, LANES), BF16),
            pltpu.VMEM((shares - 1, own_subs, rows), BF16),
            pltpu.VMEM((shares - 1,) + codebooks.shape, BF16),
            pltpu.VMEM((shares - 1,) + coarse.shape, BF16),
            pltpu.VMEM((own_subs, rows), jnp.int32),
            pltpu.VMEM((shares * own_width, rows), BF16),
            pltpu.VMEM((8, rows), F32),
            pltpu.VMEM((HALVES, total // HALVES, LANES), F32),
            pltpu.VMEM((HALVES, total // HALVES, rows), F32),
            pltpu.VMEM((HALVES, shares, 8, total // HALVES), F32),
            pltpu.VMEM((total // HALVES, width), F32),
            pltpu.VMEM((total // HALVES, LANES), F32),
            pltpu.VMEM((HALVES, shares, 8, total // HALVES), F32),
            pltpu.VMEM((HALVES, shares, groups, short, LANES), BF16),
            pltpu.VMEM((HALVES, shares - 1, groups, short, LANES), BF16),
            pltpu.VMEM((HALVES, groups, short, LANES), F32),
            pltpu.VMEM((HALVES, groups, short, LANES), F32),
            pltpu.VMEM((groups, 8, LANES), F32),
            pltpu.VMEM((groups, 8, LANES), F32),
            pltpu.VMEM((shares, width // shares, count), BF16),
            pltpu.SemaphoreType.DMA((copies,)),
            pltpu.SemaphoreType.DMA((copies,)),
        ],
        compiler_params=pltpu.CompilerParams(
            collective_id=0, has_side_effects=True, vmem_limit_bytes=56 * 1024 * 1024
        ),
    )(meta, queries, codes, codebooks, coarse, lengths, payload.reshape(rows, width))
    return pooled.T


def solution(mesh):
    placed = (
        P("cell", "sub"),
        P("cell", None),
        P("cell", None, None),
        P("cell", "sub"),
        P("sub", None, None),
        P("cell", "sub", None),
        P("cell"),
        P("cell", "sub", None),
    )
    return jax.shard_map(
        local, mesh=mesh, in_specs=placed, out_specs=P("cell", None), check_vma=False
    )
```

```python
import functools
import math

import jax
import jax.numpy as jnp
from jax import lax
from jax.experimental import pallas as pl
from jax.experimental.pallas import tpu as pltpu
from jax.sharding import PartitionSpec as P

CAP = 64
HALVES = 2
LANES = 128
score_scale = 0.3
floor_score = -1e30
F32 = jnp.float32
BF16 = jnp.bfloat16


def iota(shape, dim):
    return lax.broadcasted_iota(jnp.int32, shape, dim)


def positions(meta_ref, groups):
    count = meta_ref.shape[1]
    padded = -(-groups // 8) * 8
    group_ids = iota((padded, count), 0)
    first = (meta_ref[0:1, :] == group_ids).astype(F32)
    second = (meta_ref[1:2, :] == group_ids).astype(F32)
    routed = first + second
    before = (iota((count, count), 0) < iota((count, count), 1)).astype(F32).astype(BF16)
    earlier = jnp.dot(routed.astype(BF16), before, preferred_element_type=F32)
    return first, second, routed, earlier


def pack_kernel(groups, half, meta_ref, rows_ref, buffer_ref, away_ref):
    count = meta_ref.shape[1]
    first, second, routed, earlier = positions(meta_ref, groups)
    spot = routed * (earlier + 1.0) - 1.0
    cell_ids = iota((LANES, count), 0)

    def named(start):
        marks = jnp.zeros((LANES, count), F32)
        for k in range(half):
            marks += (meta_ref[start + k : start + k + 1, :] == cell_ids).astype(F32)
        return marks

    named_first, named_second = named(2), named(2 + half)
    ranks = iota((CAP, count), 0).astype(F32)
    for g in range(groups):
        onehot = (ranks == spot[g : g + 1, :]).astype(F32).astype(BF16)
        buffer_ref[g] = jnp.dot(
            onehot, rows_ref[...], preferred_element_type=F32
        ).astype(BF16)
        marks = first[g : g + 1, :] * named_first + second[g : g + 1, :] * named_second
        there = lax.dot_general(
            onehot, marks.astype(BF16), (((1,), (1,)), ((), ())), preferred_element_type=F32
        )
        away_ref[g] = (1.0 - there).astype(BF16)


def decode_share(subs, width, blocks, codes_ref, books_ref, base, ids, tables, centers, vectors, squares):
    near = min(8, subs)
    ids[...] = codes_ref[...].astype(F32).astype(jnp.int32)
    tables[...] = books_ref[...].astype(F32)
    for start in range(0, subs, near):

        @pl.loop(0, blocks // 2)
        def _(pair):
            for u in range(2):
                lanes = pl.ds(pl.multiple_of(pair * (2 * LANES) + u * LANES, LANES), LANES)
                inner = slice(start * width, (start + near) * width)
                around = centers[inner, lanes].astype(F32)
                found = []
                for j in range(start, start + near):
                    code = jnp.broadcast_to(ids[j : j + 1, lanes], (8, LANES))
                    index = code & (LANES - 1)
                    for d in range(0, width, 8):
                        low = tables[j, d : d + 8, :LANES]
                        high = tables[j, d : d + 8, LANES:]
                        found.append(
                            jnp.where(
                                code < LANES,
                                jnp.take_along_axis(low, index, axis=1, mode="promise_in_bounds"),
                                jnp.take_along_axis(high, index, axis=1, mode="promise_in_bounds"),
                            )
                        )
                summed = (jnp.concatenate(found, axis=0) + around).astype(BF16)
                vectors[base + start * width : base + (start + near) * width, lanes] = summed
                back = summed.astype(F32)
                back = back * back
                squares[:, lanes] += jnp.sum(back.reshape(-1, 8, LANES), axis=0)


def whole_kernel(
    groups,
    shares,
    half,
    row_local,
    fold,
    meta_ref,
    rows_ref,
    raw_codes_ref,
    books_ref,
    coarse_ref,
    lengths_ref,
    payload_ref,
    pooled_ref,
    codes_ref,
    buffer,
    away_out,
    queries,
    away,
    codes_in,
    books_in,
    coarse_in,
    ids,
    tables,
    spread,
    vectors,
    squares,
    best,
    values,
    peak_row,
    part,
    masses,
    mass_row,
    share_out,
    share_in,
    back_out,
    back_in,
    stat_out,
    stat_in,
    columns,
    send_sem,
    recv_sem,
):
    me_cell, me_sub = lax.axis_index("cell"), lax.axis_index("sub")
    count = meta_ref.shape[1]
    subs, rows = ids.shape
    book_width = books_ref.shape[1]
    cells, own_width = coarse_ref.shape
    total = groups * CAP
    width = payload_ref.shape[1]
    own_columns = width // shares
    short = CAP // fold // HALVES
    blocks = rows // LANES
    step = 512 if rows % 512 == 0 else 256
    used = [0]

    def device(cell_off, sub_off):
        return (lax.rem(me_cell + cell_off, groups), lax.rem(me_sub + sub_off, shares))

    def send(src, dst, cell_off, sub_off, target=None):
        i = used[0]
        used[0] += 1
        copy = pltpu.make_async_remote_copy(
            src_ref=src,
            dst_ref=dst,
            send_sem=send_sem.at[i],
            recv_sem=recv_sem.at[i],
            device_id=target or device(cell_off, sub_off),
            device_id_type=pl.DeviceIdType.MESH,
        )
        copy.start()
        return copy

    barrier = pltpu.get_barrier_semaphore()
    for off in range(1, groups):
        pl.semaphore_signal(
            barrier, inc=1, device_id=device(off, 0), device_id_type=pl.DeviceIdType.MESH
        )
    for off in range(1, shares):
        pl.semaphore_signal(
            barrier, inc=1, device_id=device(0, off), device_id_type=pl.DeviceIdType.MESH
        )
    several = LANES // math.gcd(row_local, LANES)
    for t in range(shares):
        for start in range(0, cells, several):
            codes_ref[t, :, start * row_local : (start + several) * row_local] = jnp.concatenate(
                [
                    raw_codes_ref[c, :, t * row_local : (t + 1) * row_local]
                    for c in range(start, start + several)
                ],
                axis=1,
            ).astype(F32).astype(BF16)
    pack_kernel(groups, half, meta_ref, rows_ref, buffer, away_out)
    pl.semaphore_wait(barrier, groups + shares - 2)

    everything = []
    routed = [None]
    for off in range(1, groups):
        target = lax.rem(me_cell + off, groups)
        routed.append(
            [
                send(buffer.at[target], queries.at[0, me_cell], off, 0),
                send(away_out.at[target], away.at[me_cell], off, 0),
            ]
        )
        everything += routed[-1]
    core = lax.rem(me_cell, 2)
    beside = (me_cell + 1 - 2 * core, me_sub)
    split = subs // 2
    mine = pl.ds(core * split, split)
    lists, halves = [None], [None]
    for off in range(1, shares):
        target = lax.rem(me_sub + off, shares)
        lists.append(
            [
                send(codes_ref.at[target], codes_in.at[off - 1], 0, off),
                send(coarse_ref, coarse_in.at[off - 1], 0, off),
            ]
        )
        halves.append(send(books_ref.at[mine], books_in.at[off - 1, mine], 0, off))
        everything.append(halves[-1])
        everything += lists[-1]

    queries[0, me_cell] = buffer[me_cell]
    away[me_cell] = away_out[me_cell]
    spread_out = []

    def forward(off):
        if off:
            for copy in routed[off]:
                copy.wait_recv()
        source = lax.rem(me_cell + groups - off, groups)
        for sub_off in range(1, shares):
            spread_out.append(
                send(queries.at[0, source], queries.at[sub_off, source], 0, sub_off)
            )

    forward(0)
    squares[...] = jnp.zeros_like(squares)
    passed = 1
    for k in range(shares):
        if k == 1:
            for off in range(1, shares):
                halves[off].wait_recv()
                here = books_in.at[off - 1, mine]
                lists[off].append(send(here, here, 0, 0, beside))
                everything.append(lists[off][-1])
        if k:
            for copy in lists[k]:
                copy.wait_recv()
        centers = coarse_in.at[k - 1] if k else coarse_ref

        @pl.loop(0, rows // step)
        def _(n):
            lanes = pl.ds(pl.multiple_of(n * step, step), step)
            shift = iota((cells, step), 1) + n * step - iota((cells, step), 0) * row_local
            inside = ((shift >= 0) & (shift < row_local)).astype(F32).astype(BF16)
            spread[:, lanes] = lax.dot_general(
                centers[...], inside, (((0,), (0,)), ((), ())), preferred_element_type=F32
            ).astype(BF16)

        decode_share(
            subs,
            book_width,
            blocks,
            codes_in.at[k - 1] if k else codes_ref.at[me_sub],
            books_in.at[k - 1] if k else books_ref,
            k * own_width,
            ids,
            tables,
            spread,
            vectors,
            squares,
        )
        until = min(groups, 1 + -(-(groups - 1) * (k + 1) // min(shares, 2)))
        for off in range(passed, until):
            forward(off)
        passed = max(passed, until)
    everything += spread_out

    offset = iota((cells, rows), 1) - iota((cells, rows), 0) * row_local
    inside = (offset >= 0) & (offset < row_local)
    reach = jnp.zeros((cells, 1), jnp.int32)
    for c in range(cells):
        reach = jnp.where(iota((cells, 1), 0) == c, lengths_ref[c], reach)
    live = jnp.sum(
        (inside & (offset + me_sub * row_local < reach)).astype(F32),
        axis=0,
        keepdims=True,
    )
    half_norm = 0.5 * jnp.sum(squares[...], axis=0, keepdims=True)
    squares[0:1, :] = jnp.where(live > 0.5, half_norm, -floor_score)
    for copy in spread_out:
        copy.wait_recv()
    part_cap = CAP // HALVES
    part_total = total // HALVES

    def score(h):
        some = slice(h * part_cap, (h + 1) * part_cap)
        best[h] = jnp.full(best.shape[1:], 3.0 * floor_score, F32)

        @pl.loop(0, rows // step)
        def _(n):
            lanes = pl.ds(pl.multiple_of(n * step, step), step)
            shift = iota((LANES, step), 1) + n * step - iota((LANES, step), 0) * row_local
            far = jnp.where((shift >= 0) & (shift < row_local), floor_score, 0.0).astype(BF16)
            raw = jnp.dot(
                away[:, some].reshape(part_total, LANES), far, preferred_element_type=F32
            )
            for k in range(shares):
                raw = raw + jnp.dot(
                    queries[k, :, some].reshape(part_total, own_width),
                    vectors[k * own_width : (k + 1) * own_width, lanes],
                    preferred_element_type=F32,
                )
            scores = (raw - squares[0:1, lanes]) * score_scale
            values[h, :, lanes] = scores
            top = best[h]
            for b in range(step // LANES):
                top = jnp.maximum(top, scores[:, b * LANES : (b + 1) * LANES])
            best[h] = top

        peak_row[h, 0] = jnp.broadcast_to(
            jnp.max(jnp.transpose(best[h]), axis=0, keepdims=True), (8, part_total)
        )
        return [
            send(peak_row.at[h, 0], peak_row.at[h, off], 0, off) for off in range(1, shares)
        ]

    def pool(h, tops):
        for copy in tops:
            copy.wait_recv()
        peak = jnp.max(peak_row[h], axis=0)
        best[h] = jnp.transpose(jnp.broadcast_to(peak[0:1], (LANES, part_total)))
        part[...] = jnp.zeros_like(part)
        masses[...] = jnp.zeros_like(masses)

        @pl.loop(0, rows // step)
        def _(n):
            lanes = pl.ds(pl.multiple_of(n * step, step), step)
            mass = masses[...]
            pieces = []
            for b in range(step // LANES):
                inner = pl.ds(pl.multiple_of(n * step + b * LANES, LANES), LANES)
                piece = jnp.exp(values[h, :, inner] - best[h]).astype(BF16)
                mass = mass + piece.astype(F32)
                pieces.append(piece)
            masses[...] = mass
            part[...] += jnp.dot(
                jnp.concatenate(pieces, axis=1),
                payload_ref[lanes, :],
                preferred_element_type=F32,
            )

        mass_row[h, 0] = jnp.broadcast_to(
            jnp.sum(jnp.transpose(masses[...]), axis=0, keepdims=True), (8, part_total)
        )
        sums = part[...].reshape(groups, part_cap, width)
        for t in range(shares):
            own = slice(t * own_columns, (t + 1) * own_columns)
            share_out[h, t] = jnp.concatenate(
                [sums[:, b * short : (b + 1) * short, own] for b in range(fold)], axis=2
            ).astype(share_out.dtype)
        shared = []
        for off in range(1, shares):
            target = lax.rem(me_sub + off, shares)
            shared.append(send(share_out.at[h, target], share_in.at[h, off - 1], 0, off))
            shared.append(send(mass_row.at[h, 0], mass_row.at[h, off], 0, off))
        return shared, peak

    def give_back(h, shared, peak):
        for copy in shared:
            copy.wait_recv()
        share = share_out[h, me_sub].astype(F32)
        for off in range(1, shares):
            share = share + share_in[h, off - 1].astype(F32)
        back_out[h] = share
        sent = []
        for off in range(1, groups):
            target = lax.rem(me_cell + off, groups)
            sent.append(send(back_out.at[h, target], back_in.at[h, me_cell], off, 0))
        back_in[h, me_cell] = back_out[h, me_cell]
        mass_all = mass_row[h, 0]
        for off in range(1, shares):
            mass_all = mass_all + mass_row[h, off]
        return sent, jnp.where(iota((8, part_total), 0) == 0, mass_all, peak)

    tops = [score(h) for h in range(HALVES)]
    pooled = [pool(h, tops[h]) for h in range(HALVES)]
    given = [give_back(h, *pooled[h]) for h in range(HALVES)]
    returned = []
    for h in range(HALVES):
        everything += tops[h] + pooled[h][0] + given[h][0]
        returned += given[h][0]
    for g in range(groups):
        mine = [stats[:, g * part_cap : (g + 1) * part_cap] for _, stats in given]
        stat_out[g] = jnp.concatenate(mine + [jnp.zeros((8, LANES - CAP), F32)], axis=1)
    stat_sent = []
    for off in range(1, groups):
        target = lax.rem(me_cell + off, groups)
        stat_sent.append(send(stat_out.at[target], stat_in.at[me_cell], off, 0))
    everything += stat_sent
    returned += stat_sent
    stat_in[me_cell] = stat_out[me_cell]

    first, second, _, earlier = positions(meta_ref, groups)
    marks = []
    for route, named in ((0, first), (1, second)):
        spot = jnp.sum(
            named * earlier, axis=0, keepdims=True
        ).astype(jnp.int32)
        slot = meta_ref[route : route + 1, :] * CAP + spot
        marks.append((iota((total, count), 0) == slot).astype(F32).astype(BF16))
    for copy in returned:
        copy.wait_recv()

    def pick(array, mark, dim):
        out = 0.0
        for _ in range(3):
            piece = array.astype(BF16)
            out = out + lax.dot_general(
                piece, mark, (((dim,), (0,)), ((), ())), preferred_element_type=F32
            )
            array = array - piece.astype(F32)
        return out

    table = jnp.concatenate(
        [
            back_in[h][:, :, b * own_columns : (b + 1) * own_columns]
            for h in range(HALVES)
            for b in range(fold)
        ],
        axis=1,
    ).reshape(total, own_columns)
    stat_row = jnp.concatenate([stat_in[g][:, :CAP] for g in range(groups)], axis=1)
    stat_0, stat_1 = pick(stat_row, marks[0], 1), pick(stat_row, marks[1], 1)
    top = jnp.maximum(stat_0[1:2], stat_1[1:2])
    scale_0, scale_1 = jnp.exp(stat_0[1:2] - top), jnp.exp(stat_1[1:2] - top)
    lower = scale_0 * stat_0[0:1] + scale_1 * stat_1[0:1]
    upper = scale_0 * pick(table, marks[0], 0) + scale_1 * pick(table, marks[1], 0)
    columns[me_sub] = (upper / lower).astype(BF16)
    gathered = [
        send(columns.at[me_sub], columns.at[me_sub], 0, off) for off in range(1, shares)
    ]
    everything += gathered
    for copy in gathered:
        copy.wait_recv()
    pooled_ref[...] = columns[...].reshape(width, count)
    for copy in everything:
        copy.wait_send()


def local(queries, probe_groups, probe_cells, coarse, codebooks, codes, lengths, payload):
    groups, shares = lax.axis_size("cell"), lax.axis_size("sub")
    count, own_width = queries.shape
    half = probe_cells.shape[2]
    cells, own_subs, row_slots = codes.shape
    row_local = row_slots // shares
    rows = cells * row_local
    total = groups * CAP
    width = payload.shape[2]
    fold = LANES // (width // shares)
    short = CAP // fold // HALVES
    meta = jnp.concatenate([probe_groups, probe_cells.reshape(count, -1)], axis=1).T
    copies = (3 + HALVES) * (groups - 1) + (groups + 5 + 3 * HALVES) * (shares - 1)
    spec = pl.BlockSpec(memory_space=pltpu.VMEM)
    pooled = pl.pallas_call(
        functools.partial(whole_kernel, groups, shares, half, row_local, fold),
        out_shape=jax.ShapeDtypeStruct((width, count), BF16),
        in_specs=[spec] * 5 + [pl.BlockSpec(memory_space=pltpu.SMEM), spec],
        out_specs=spec,
        scratch_shapes=[
            pltpu.VMEM((shares, own_subs, rows), BF16),
            pltpu.VMEM((groups, CAP, own_width), BF16),
            pltpu.VMEM((groups, CAP, LANES), BF16),
            pltpu.VMEM((shares, groups, CAP, own_width), BF16),
            pltpu.VMEM((groups, CAP, LANES), BF16),
            pltpu.VMEM((shares - 1, own_subs, rows), BF16),
            pltpu.VMEM((shares - 1,) + codebooks.shape, BF16),
            pltpu.VMEM((shares - 1,) + coarse.shape, BF16),
            pltpu.VMEM((own_subs, rows), jnp.int32),
            pltpu.VMEM(codebooks.shape, F32),
            pltpu.VMEM((own_width, rows), BF16),
            pltpu.VMEM((shares * own_width, rows), BF16),
            pltpu.VMEM((8, rows), F32),
            pltpu.VMEM((HALVES, total // HALVES, LANES), F32),
            pltpu.VMEM((HALVES, total // HALVES, rows), F32),
            pltpu.VMEM((HALVES, shares, 8, total // HALVES), F32),
            pltpu.VMEM((total // HALVES, width), F32),
            pltpu.VMEM((total // HALVES, LANES), F32),
            pltpu.VMEM((HALVES, shares, 8, total // HALVES), F32),
            pltpu.VMEM((HALVES, shares, groups, short, LANES), F32),
            pltpu.VMEM((HALVES, shares - 1, groups, short, LANES), F32),
            pltpu.VMEM((HALVES, groups, short, LANES), F32),
            pltpu.VMEM((HALVES, groups, short, LANES), F32),
            pltpu.VMEM((groups, 8, LANES), F32),
            pltpu.VMEM((groups, 8, LANES), F32),
            pltpu.VMEM((shares, width // shares, count), BF16),
            pltpu.SemaphoreType.DMA((copies,)),
            pltpu.SemaphoreType.DMA((copies,)),
        ],
        compiler_params=pltpu.CompilerParams(
            collective_id=0, has_side_effects=True, vmem_limit_bytes=56 * 1024 * 1024
        ),
    )(meta, queries, codes, codebooks, coarse, lengths, payload.reshape(rows, width))
    return pooled.T


def solution(mesh):
    placed = (
        P("cell", "sub"),
        P("cell", None),
        P("cell", None, None),
        P("cell", "sub"),
        P("sub", None, None),
        P("cell", "sub", None),
        P("cell"),
        P("cell", "sub", None),
    )
    return jax.shard_map(
        local, mesh=mesh, in_specs=placed, out_specs=P("cell", None), check_vma=False
    )
```

```python
import functools
import math

import jax
import jax.numpy as jnp
from jax import lax
from jax.experimental import pallas as pl
from jax.experimental.pallas import tpu as pltpu
from jax.sharding import PartitionSpec as P

CAP = 64
HALVES = 2
LANES = 128
score_scale = 0.3
floor_score = -1e30
F32 = jnp.float32
BF16 = jnp.bfloat16


def iota(shape, dim):
    return lax.broadcasted_iota(jnp.int32, shape, dim)


def positions(meta_ref, groups):
    count = meta_ref.shape[1]
    padded = -(-groups // 8) * 8
    group_ids = iota((padded, count), 0)
    first = (meta_ref[0:1, :] == group_ids).astype(F32)
    second = (meta_ref[1:2, :] == group_ids).astype(F32)
    routed = first + second
    before = (iota((count, count), 0) < iota((count, count), 1)).astype(F32).astype(BF16)
    earlier = jnp.dot(routed.astype(BF16), before, preferred_element_type=F32)
    return first, second, routed, earlier


def pack_kernel(groups, half, cells, meta_ref, rows_ref, buffer_ref, away_ref):
    count = meta_ref.shape[1]
    first, second, routed, earlier = positions(meta_ref, groups)
    spot = routed * (earlier + 1.0) - 1.0
    cell_ids = lax.rem(iota((LANES, count), 0), cells)
    folds = LANES // cells
    short = CAP // folds
    lane_group = iota((short, LANES), 1) // cells

    def named(start):
        marks = jnp.zeros((LANES, count), F32)
        for k in range(half):
            marks += (meta_ref[start + k : start + k + 1, :] == cell_ids).astype(F32)
        return marks

    named_first, named_second = named(2), named(2 + half)
    ranks = iota((CAP, count), 0).astype(F32)
    for g in range(groups):
        onehot = (ranks == spot[g : g + 1, :]).astype(F32).astype(BF16)
        buffer_ref[g] = jnp.dot(
            onehot, rows_ref[...], preferred_element_type=F32
        ).astype(BF16)
        marks = first[g : g + 1, :] * named_first + second[g : g + 1, :] * named_second
        there = lax.dot_general(
            onehot, marks.astype(BF16), (((1,), (1,)), ((), ())), preferred_element_type=F32
        )
        packed = jnp.zeros((short, LANES), F32)
        for b in range(folds):
            packed = jnp.where(lane_group == b, there[b * short : (b + 1) * short], packed)
        away_ref[g] = (1.0 - packed).astype(BF16)


def look_up(table, index):
    along = lax.GatherDimensionNumbers(
        offset_dims=(),
        collapsed_slice_dims=(1,),
        start_index_map=(1,),
        operand_batching_dims=(0,),
        start_indices_batching_dims=(0,),
    )
    return lax.gather(
        table,
        index[..., None],
        along,
        slice_sizes=(1, 1),
        mode=lax.GatherScatterMode.PROMISE_IN_BOUNDS,
    )


def decode_share(between, subs, width, blocks, codes_ref, books_ref, base, ids, centers, vectors, squares):
    near = min(8, subs)
    ids[...] = codes_ref[...].astype(F32).astype(jnp.int32)
    for start in range(0, subs, near):
        between()

        @pl.loop(0, blocks // 2)
        def _(pair):
            for u in range(2):
                lanes = pl.ds(pl.multiple_of(pair * (2 * LANES) + u * LANES, LANES), LANES)
                inner = slice(start * width, (start + near) * width)
                around = centers[inner, lanes]
                found = []
                for j in range(start, start + near):
                    code = jnp.broadcast_to(ids[j : j + 1, lanes], (width, LANES)).astype(jnp.int16)
                    index = code & (LANES - 1)
                    found.append(
                        jnp.where(
                            code < LANES,
                            look_up(books_ref[j, :, :LANES], index),
                            look_up(books_ref[j, :, LANES:], index),
                        )
                    )
                summed = jnp.concatenate(found, axis=0) + around
                vectors[base + start * width : base + (start + near) * width, lanes] = summed
                back = summed.astype(F32)
                back = back * back
                squares[:, lanes] += jnp.sum(back.reshape(-1, 8, LANES), axis=0)


def whole_kernel(
    groups,
    shares,
    half,
    row_local,
    fold,
    meta_ref,
    rows_ref,
    raw_codes_ref,
    books_ref,
    coarse_ref,
    lengths_ref,
    payload_hbm,
    pooled_ref,
    payload_ref,
    payload_sem,
    codes_ref,
    buffer,
    away_out,
    queries,
    away_in,
    away,
    codes_in,
    books_in,
    coarse_in,
    ids,
    spread,
    vectors,
    squares,
    best,
    values,
    peak_row,
    part,
    masses,
    mass_row,
    share_out,
    share_in,
    back_out,
    back_in,
    stat_out,
    stat_in,
    columns,
    send_sem,
    recv_sem,
):
    me_cell, me_sub = lax.axis_index("cell"), lax.axis_index("sub")
    count = meta_ref.shape[1]
    subs, rows = ids.shape
    book_width = books_ref.shape[1]
    cells, own_width = coarse_ref.shape
    total = groups * CAP
    width = payload_hbm.shape[1]
    own_columns = width // shares
    short = CAP // fold // HALVES
    blocks = rows // LANES
    step = 512 if rows % 512 == 0 else 256
    used = [0]

    def device(cell_off, sub_off):
        return (lax.rem(me_cell + cell_off, groups), lax.rem(me_sub + sub_off, shares))

    def send(src, dst, cell_off, sub_off, target=None):
        i = used[0]
        used[0] += 1
        copy = pltpu.make_async_remote_copy(
            src_ref=src,
            dst_ref=dst,
            send_sem=send_sem.at[i],
            recv_sem=recv_sem.at[i],
            device_id=target or device(cell_off, sub_off),
            device_id_type=pl.DeviceIdType.MESH,
        )
        copy.start()
        return copy

    barrier = pltpu.get_barrier_semaphore()
    table_copy = pltpu.make_async_copy(payload_hbm, payload_ref, payload_sem)
    table_copy.start()
    for off in range(1, groups):
        pl.semaphore_signal(
            barrier, inc=1, device_id=device(off, 0), device_id_type=pl.DeviceIdType.MESH
        )
    for off in range(1, shares):
        pl.semaphore_signal(
            barrier, inc=1, device_id=device(0, off), device_id_type=pl.DeviceIdType.MESH
        )
    pack_kernel(groups, half, cells, meta_ref, rows_ref, buffer, away_out)
    pl.semaphore_wait(barrier, groups + shares - 2)

    everything = []
    routed = [None]
    for off in range(1, groups):
        target = lax.rem(me_cell + off, groups)
        routed.append(
            [
                send(buffer.at[target], queries.at[0, me_cell], off, 0),
                send(away_out.at[target], away_in.at[me_cell], off, 0),
            ]
        )
        everything += routed[-1]
    several = LANES // math.gcd(row_local, LANES)
    for t in range(shares):
        for start in range(0, cells, several):
            codes_ref[t, :, start * row_local : (start + several) * row_local] = jnp.concatenate(
                [
                    raw_codes_ref[c, :, t * row_local : (t + 1) * row_local]
                    for c in range(start, start + several)
                ],
                axis=1,
            ).astype(F32).astype(BF16)
    core = lax.rem(me_cell, 2)
    beside = (me_cell + 1 - 2 * core, me_sub)
    split = subs // 2
    mine = pl.ds(core * split, split)
    lists, halves = [None], [None]
    for off in range(1, shares):
        target = lax.rem(me_sub + off, shares)
        lists.append(
            [
                send(codes_ref.at[target], codes_in.at[off - 1], 0, off),
                send(coarse_ref, coarse_in.at[off - 1], 0, off),
            ]
        )
        halves.append(send(books_ref.at[mine], books_in.at[off - 1, mine], 0, off))
        everything.append(halves[-1])
        everything += lists[-1]

    queries[0, me_cell] = buffer[me_cell]
    away_in[me_cell] = away_out[me_cell]
    spread_out = []

    def forward(off):
        if off:
            for copy in routed[off]:
                copy.wait_recv()
        source = lax.rem(me_cell + groups - off, groups)
        for sub_off in range(1, shares):
            spread_out.append(
                send(queries.at[0, source], queries.at[sub_off, source], 0, sub_off)
            )

    forward(0)
    squares[...] = jnp.zeros_like(squares)
    waiting = sorted(range(1, groups), key=lambda off: min(off, groups - off))
    pauses = [0]

    def between():
        if pauses[0] and waiting:
            forward(waiting.pop(0))
        pauses[0] += 1

    for k in range(shares):
        if k == 1:
            for off in range(1, shares):
                halves[off].wait_recv()
                here = books_in.at[off - 1, mine]
                lists[off].append(send(here, here, 0, 0, beside))
                everything.append(lists[off][-1])
        if k:
            for copy in lists[k]:
                copy.wait_recv()
        centers = coarse_in.at[k - 1] if k else coarse_ref

        @pl.loop(0, rows // step)
        def _(n):
            lanes = pl.ds(pl.multiple_of(n * step, step), step)
            shift = iota((cells, step), 1) + n * step - iota((cells, step), 0) * row_local
            inside = ((shift >= 0) & (shift < row_local)).astype(F32).astype(BF16)
            spread[:, lanes] = lax.dot_general(
                centers[...], inside, (((0,), (0,)), ((), ())), preferred_element_type=F32
            ).astype(BF16)

        decode_share(
            between,
            subs,
            book_width,
            blocks,
            codes_in.at[k - 1] if k else codes_ref.at[me_sub],
            books_in.at[k - 1] if k else books_ref,
            k * own_width,
            ids,
            spread,
            vectors,
            squares,
        )
    while waiting:
        forward(waiting.pop(0))
    everything += spread_out

    offset = iota((cells, rows), 1) - iota((cells, rows), 0) * row_local
    inside = (offset >= 0) & (offset < row_local)
    reach = jnp.zeros((cells, 1), jnp.int32)
    for c in range(cells):
        reach = jnp.where(iota((cells, 1), 0) == c, lengths_ref[c], reach)
    live = jnp.sum(
        (inside & (offset + me_sub * row_local < reach)).astype(F32),
        axis=0,
        keepdims=True,
    )
    half_norm = 0.5 * jnp.sum(squares[...], axis=0, keepdims=True)
    squares[0:1, :] = jnp.where(live > 0.5, half_norm, -floor_score)
    for copy in spread_out:
        copy.wait_recv()
    folds = LANES // cells
    deep = CAP // folds
    lane_group = iota((groups, deep, LANES), 2) // cells
    packed = away_in[...].astype(F32)
    for b in range(folds):
        away[:, b * deep : (b + 1) * deep] = jnp.where(lane_group == b, packed, 0.0).astype(BF16)
    part_cap = CAP // HALVES
    part_total = total // HALVES

    def score(h):
        some = slice(h * part_cap, (h + 1) * part_cap)
        best[h] = jnp.full(best.shape[1:], 3.0 * floor_score, F32)

        @pl.loop(0, rows // step)
        def _(n):
            lanes = pl.ds(pl.multiple_of(n * step, step), step)
            cell_of = lax.rem(iota((LANES, step), 0), cells)
            shift = iota((LANES, step), 1) + n * step - cell_of * row_local
            far = jnp.where((shift >= 0) & (shift < row_local), floor_score, 0.0).astype(BF16)
            raw = jnp.dot(
                away[:, some].reshape(part_total, LANES), far, preferred_element_type=F32
            )
            for k in range(shares):
                raw = raw + jnp.dot(
                    queries[k, :, some].reshape(part_total, own_width),
                    vectors[k * own_width : (k + 1) * own_width, lanes],
                    preferred_element_type=F32,
                )
            scores = (raw - squares[0:1, lanes]) * score_scale
            values[h, :, lanes] = scores
            top = best[h]
            for b in range(step // LANES):
                top = jnp.maximum(top, scores[:, b * LANES : (b + 1) * LANES])
            best[h] = top

        peak_row[h, 0] = jnp.broadcast_to(
            jnp.max(jnp.transpose(best[h]), axis=0, keepdims=True), (8, part_total)
        )
        return [
            send(peak_row.at[h, 0], peak_row.at[h, off], 0, off) for off in range(1, shares)
        ]

    def pool(h, tops):
        for copy in tops:
            copy.wait_recv()
        peak = jnp.max(peak_row[h], axis=0)
        best[h] = jnp.transpose(jnp.broadcast_to(peak[0:1], (LANES, part_total)))
        part[...] = jnp.zeros_like(part)
        masses[...] = jnp.zeros_like(masses)

        @pl.loop(0, rows // step)
        def _(n):
            lanes = pl.ds(pl.multiple_of(n * step, step), step)
            mass = masses[...]
            pieces = []
            for b in range(step // LANES):
                inner = pl.ds(pl.multiple_of(n * step + b * LANES, LANES), LANES)
                piece = jnp.exp(values[h, :, inner] - best[h]).astype(BF16)
                mass = mass + piece.astype(F32)
                pieces.append(piece)
            masses[...] = mass
            part[...] += jnp.dot(
                jnp.concatenate(pieces, axis=1),
                payload_ref[lanes, :],
                preferred_element_type=F32,
            )

        mass_row[h, 0] = jnp.broadcast_to(
            jnp.sum(jnp.transpose(masses[...]), axis=0, keepdims=True), (8, part_total)
        )
        sums = part[...].reshape(groups, part_cap, width)
        for t in range(shares):
            own = slice(t * own_columns, (t + 1) * own_columns)
            share_out[h, t] = jnp.concatenate(
                [sums[:, b * short : (b + 1) * short, own] for b in range(fold)], axis=2
            ).astype(share_out.dtype)
        shared = []
        for off in range(1, shares):
            target = lax.rem(me_sub + off, shares)
            shared.append(send(share_out.at[h, target], share_in.at[h, off - 1], 0, off))
            shared.append(send(mass_row.at[h, 0], mass_row.at[h, off], 0, off))
        return shared, peak

    def give_back(h, shared, peak):
        for copy in shared:
            copy.wait_recv()
        share = share_out[h, me_sub].astype(F32)
        for off in range(1, shares):
            share = share + share_in[h, off - 1].astype(F32)
        back_out[h] = share
        sent = []
        for off in range(1, groups):
            target = lax.rem(me_cell + off, groups)
            sent.append(send(back_out.at[h, target], back_in.at[h, me_cell], off, 0))
        back_in[h, me_cell] = back_out[h, me_cell]
        mass_all = mass_row[h, 0]
        for off in range(1, shares):
            mass_all = mass_all + mass_row[h, off]
        return sent, jnp.where(iota((8, part_total), 0) == 0, mass_all, peak)

    tops = [score(h) for h in range(HALVES)]
    table_copy.wait()
    pooled = [pool(h, tops[h]) for h in range(HALVES)]
    given = [give_back(h, *pooled[h]) for h in range(HALVES)]
    returned = []
    for h in range(HALVES):
        everything += tops[h] + pooled[h][0] + given[h][0]
        returned += given[h][0]
    for g in range(groups):
        mine = [stats[:, g * part_cap : (g + 1) * part_cap] for _, stats in given]
        stat_out[g] = jnp.concatenate(mine + [jnp.zeros((8, LANES - CAP), F32)], axis=1)
    stat_sent = []
    for off in range(1, groups):
        target = lax.rem(me_cell + off, groups)
        stat_sent.append(send(stat_out.at[target], stat_in.at[me_cell], off, 0))
    everything += stat_sent
    returned += stat_sent
    stat_in[me_cell] = stat_out[me_cell]

    first, second, _, earlier = positions(meta_ref, groups)
    marks = []
    for route, named in ((0, first), (1, second)):
        spot = jnp.sum(
            named * earlier, axis=0, keepdims=True
        ).astype(jnp.int32)
        slot = meta_ref[route : route + 1, :] * CAP + spot
        marks.append((iota((total, count), 0) == slot).astype(F32).astype(BF16))
    for copy in returned:
        copy.wait_recv()

    def pick(array, mark, dim):
        out = 0.0
        for _ in range(3):
            piece = array.astype(BF16)
            out = out + lax.dot_general(
                piece, mark, (((dim,), (0,)), ((), ())), preferred_element_type=F32
            )
            array = array - piece.astype(F32)
        return out

    table = jnp.concatenate(
        [
            back_in[h][:, :, b * own_columns : (b + 1) * own_columns]
            for h in range(HALVES)
            for b in range(fold)
        ],
        axis=1,
    ).reshape(total, own_columns)
    stat_row = jnp.concatenate([stat_in[g][:, :CAP] for g in range(groups)], axis=1)
    stat_0, stat_1 = pick(stat_row, marks[0], 1), pick(stat_row, marks[1], 1)
    top = jnp.maximum(stat_0[1:2], stat_1[1:2])
    scale_0, scale_1 = jnp.exp(stat_0[1:2] - top), jnp.exp(stat_1[1:2] - top)
    lower = scale_0 * stat_0[0:1] + scale_1 * stat_1[0:1]
    upper = scale_0 * pick(table, marks[0], 0) + scale_1 * pick(table, marks[1], 0)
    columns[me_sub] = (upper / lower).astype(BF16)
    gathered = [
        send(columns.at[me_sub], columns.at[me_sub], 0, off) for off in range(1, shares)
    ]
    everything += gathered
    for copy in gathered:
        copy.wait_recv()
    pooled_ref[...] = columns[...].reshape(width, count)
    for copy in everything:
        copy.wait_send()


def local(queries, probe_groups, probe_cells, coarse, codebooks, codes, lengths, payload):
    groups, shares = lax.axis_size("cell"), lax.axis_size("sub")
    count, own_width = queries.shape
    half = probe_cells.shape[2]
    cells, own_subs, row_slots = codes.shape
    row_local = row_slots // shares
    rows = cells * row_local
    total = groups * CAP
    width = payload.shape[2]
    fold = LANES // (width // shares)
    short = CAP // fold // HALVES
    meta = jnp.concatenate([probe_groups, probe_cells.reshape(count, -1)], axis=1).T
    copies = (3 + HALVES) * (groups - 1) + (groups + 5 + 3 * HALVES) * (shares - 1)
    spec = pl.BlockSpec(memory_space=pltpu.VMEM)
    pooled = pl.pallas_call(
        functools.partial(whole_kernel, groups, shares, half, row_local, fold),
        out_shape=jax.ShapeDtypeStruct((width, count), BF16),
        in_specs=[spec] * 5 + [pl.BlockSpec(memory_space=pltpu.SMEM), pl.BlockSpec(memory_space=pl.ANY)],
        out_specs=spec,
        scratch_shapes=[
            pltpu.VMEM((rows, width), BF16),
            pltpu.SemaphoreType.DMA,
            pltpu.VMEM((shares, own_subs, rows), BF16),
            pltpu.VMEM((groups, CAP, own_width), BF16),
            pltpu.VMEM((groups, CAP * cells // LANES, LANES), BF16),
            pltpu.VMEM((shares, groups, CAP, own_width), BF16),
            pltpu.VMEM((groups, CAP * cells // LANES, LANES), BF16),
            pltpu.VMEM((groups, CAP, LANES), BF16),
            pltpu.VMEM((shares - 1, own_subs, rows), BF16),
            pltpu.VMEM((shares - 1,) + codebooks.shape, BF16),
            pltpu.VMEM((shares - 1,) + coarse.shape, BF16),
            pltpu.VMEM((own_subs, rows), jnp.int32),
            pltpu.VMEM((own_width, rows), BF16),
            pltpu.VMEM((shares * own_width, rows), BF16),
            pltpu.VMEM((8, rows), F32),
            pltpu.VMEM((HALVES, total // HALVES, LANES), F32),
            pltpu.VMEM((HALVES, total // HALVES, rows), F32),
            pltpu.VMEM((HALVES, shares, 8, total // HALVES), F32),
            pltpu.VMEM((total // HALVES, width), F32),
            pltpu.VMEM((total // HALVES, LANES), F32),
            pltpu.VMEM((HALVES, shares, 8, total // HALVES), F32),
            pltpu.VMEM((HALVES, shares, groups, short, LANES), F32),
            pltpu.VMEM((HALVES, shares - 1, groups, short, LANES), F32),
            pltpu.VMEM((HALVES, groups, short, LANES), F32),
            pltpu.VMEM((HALVES, groups, short, LANES), F32),
            pltpu.VMEM((groups, 8, LANES), F32),
            pltpu.VMEM((groups, 8, LANES), F32),
            pltpu.VMEM((shares, width // shares, count), BF16),
            pltpu.SemaphoreType.DMA((copies,)),
            pltpu.SemaphoreType.DMA((copies,)),
        ],
        compiler_params=pltpu.CompilerParams(
            collective_id=0, has_side_effects=True, vmem_limit_bytes=56 * 1024 * 1024
        ),
    )(meta, queries, codes, codebooks, coarse, lengths, payload.reshape(rows, width))
    return pooled.T


def solution(mesh):
    placed = (
        P("cell", "sub"),
        P("cell", None),
        P("cell", None, None),
        P("cell", "sub"),
        P("sub", None, None),
        P("cell", "sub", None),
        P("cell"),
        P("cell", "sub", None),
    )
    return jax.shard_map(
        local, mesh=mesh, in_specs=placed, out_specs=P("cell", None), check_vma=False
    )
```

```python
import functools
import math

import jax
import jax.numpy as jnp
from jax import lax
from jax.experimental import pallas as pl
from jax.experimental.pallas import tpu as pltpu
from jax.sharding import PartitionSpec as P

CAP = 64
HALVES = 2
LANES = 128
score_scale = 0.3
floor_score = -1e30
F32 = jnp.float32
BF16 = jnp.bfloat16


def iota(shape, dim):
    return lax.broadcasted_iota(jnp.int32, shape, dim)


def positions(meta_ref, groups):
    count = meta_ref.shape[1]
    padded = -(-groups // 8) * 8
    group_ids = iota((padded, count), 0)
    first = (meta_ref[0:1, :] == group_ids).astype(F32)
    second = (meta_ref[1:2, :] == group_ids).astype(F32)
    routed = first + second
    before = (iota((count, count), 0) < iota((count, count), 1)).astype(F32).astype(BF16)
    earlier = jnp.dot(routed.astype(BF16), before, preferred_element_type=F32)
    return first, second, routed, earlier


def pack_kernel(groups, half, cells, meta_ref, rows_ref, buffer_ref, away_ref):
    count = meta_ref.shape[1]
    first, second, routed, earlier = positions(meta_ref, groups)
    spot = routed * (earlier + 1.0) - 1.0
    cell_ids = lax.rem(iota((LANES, count), 0), cells)
    folds = LANES // cells
    short = CAP // folds
    lane_group = iota((short, LANES), 1) // cells

    def named(start):
        marks = jnp.zeros((LANES, count), F32)
        for k in range(half):
            marks += (meta_ref[start + k : start + k + 1, :] == cell_ids).astype(F32)
        return marks

    named_first, named_second = named(2), named(2 + half)
    ranks = iota((CAP, count), 0).astype(F32)
    for g in range(groups):
        onehot = (ranks == spot[g : g + 1, :]).astype(F32).astype(BF16)
        buffer_ref[g] = jnp.dot(
            onehot, rows_ref[...], preferred_element_type=F32
        ).astype(BF16)
        marks = first[g : g + 1, :] * named_first + second[g : g + 1, :] * named_second
        there = lax.dot_general(
            onehot, marks.astype(BF16), (((1,), (1,)), ((), ())), preferred_element_type=F32
        )
        packed = jnp.zeros((short, LANES), F32)
        for b in range(folds):
            packed = jnp.where(lane_group == b, there[b * short : (b + 1) * short], packed)
        away_ref[g] = (1.0 - packed).astype(BF16)


def look_up(table, index):
    along = lax.GatherDimensionNumbers(
        offset_dims=(),
        collapsed_slice_dims=(1,),
        start_index_map=(1,),
        operand_batching_dims=(0,),
        start_indices_batching_dims=(0,),
    )
    return lax.gather(
        table,
        index[..., None],
        along,
        slice_sizes=(1, 1),
        mode=lax.GatherScatterMode.PROMISE_IN_BOUNDS,
    )


def decode_share(between, subs, width, blocks, codes_ref, books_ref, base, ids, centers, vectors, squares):
    near = min(8, subs)
    ids[...] = codes_ref[...].astype(F32).astype(jnp.int32)
    for start in range(0, subs, near):
        between()

        @pl.loop(0, blocks // 2)
        def _(pair):
            for u in range(2):
                lanes = pl.ds(pl.multiple_of(pair * (2 * LANES) + u * LANES, LANES), LANES)
                inner = slice(start * width, (start + near) * width)
                around = centers[inner, lanes]
                found = []
                for j in range(start, start + near):
                    code = jnp.broadcast_to(ids[j : j + 1, lanes], (width, LANES)).astype(jnp.int16)
                    index = code & (LANES - 1)
                    found.append(
                        jnp.where(
                            code < LANES,
                            look_up(books_ref[j, :, :LANES], index),
                            look_up(books_ref[j, :, LANES:], index),
                        )
                    )
                summed = jnp.concatenate(found, axis=0) + around
                vectors[base + start * width : base + (start + near) * width, lanes] = summed
                back = summed.astype(F32)
                back = back * back
                squares[:, lanes] += jnp.sum(back.reshape(-1, 8, LANES), axis=0)


def whole_kernel(
    groups,
    shares,
    half,
    row_local,
    fold,
    meta_ref,
    rows_ref,
    raw_codes_ref,
    books_ref,
    coarse_ref,
    lengths_ref,
    payload_hbm,
    pooled_ref,
    payload_ref,
    payload_sem,
    codes_ref,
    buffer,
    away_out,
    queries,
    away_in,
    away,
    codes_in,
    books_in,
    coarse_in,
    ids,
    spread,
    joined,
    vectors,
    squares,
    best,
    values,
    peak_row,
    part,
    masses,
    mass_row,
    share_out,
    share_in,
    back_out,
    back_in,
    stat_out,
    stat_in,
    columns,
    send_sem,
    recv_sem,
):
    me_cell, me_sub = lax.axis_index("cell"), lax.axis_index("sub")
    count = meta_ref.shape[1]
    subs, rows = ids.shape
    book_width = books_ref.shape[1]
    cells, own_width = coarse_ref.shape
    total = groups * CAP
    width = payload_hbm.shape[1]
    own_columns = width // shares
    short = CAP // fold // HALVES
    blocks = rows // LANES
    step = 512 if rows % 512 == 0 else 256
    used = [0]

    def device(cell_off, sub_off):
        return (lax.rem(me_cell + cell_off, groups), lax.rem(me_sub + sub_off, shares))

    def send(src, dst, cell_off, sub_off, target=None):
        i = used[0]
        used[0] += 1
        copy = pltpu.make_async_remote_copy(
            src_ref=src,
            dst_ref=dst,
            send_sem=send_sem.at[i],
            recv_sem=recv_sem.at[i],
            device_id=target or device(cell_off, sub_off),
            device_id_type=pl.DeviceIdType.MESH,
        )
        copy.start()
        return copy

    barrier = pltpu.get_barrier_semaphore()
    table_copy = pltpu.make_async_copy(payload_hbm, payload_ref, payload_sem)
    table_copy.start()
    for off in range(1, groups):
        pl.semaphore_signal(
            barrier, inc=1, device_id=device(off, 0), device_id_type=pl.DeviceIdType.MESH
        )
    for off in range(1, shares):
        pl.semaphore_signal(
            barrier, inc=1, device_id=device(0, off), device_id_type=pl.DeviceIdType.MESH
        )
    pack_kernel(groups, half, cells, meta_ref, rows_ref, buffer, away_out)
    pl.semaphore_wait(barrier, groups + shares - 2)

    everything = []
    routed = [None]
    for off in range(1, groups):
        target = lax.rem(me_cell + off, groups)
        routed.append(
            [
                send(buffer.at[target], queries.at[0, me_cell], off, 0),
                send(away_out.at[target], away_in.at[me_cell], off, 0),
            ]
        )
        everything += routed[-1]
    several = LANES // math.gcd(row_local, LANES)
    for t in range(shares):
        for start in range(0, cells, several):
            codes_ref[t, :, start * row_local : (start + several) * row_local] = jnp.concatenate(
                [
                    raw_codes_ref[c, :, t * row_local : (t + 1) * row_local]
                    for c in range(start, start + several)
                ],
                axis=1,
            ).astype(F32).astype(BF16)
    core = lax.rem(me_cell, 2)
    beside = (me_cell + 1 - 2 * core, me_sub)
    split = subs // 2
    mine = pl.ds(core * split, split)
    lists, halves = [None], [None]
    for off in range(1, shares):
        target = lax.rem(me_sub + off, shares)
        lists.append(
            [
                send(codes_ref.at[target], codes_in.at[off - 1], 0, off),
                send(coarse_ref, coarse_in.at[off - 1], 0, off),
            ]
        )
        halves.append(send(books_ref.at[mine], books_in.at[off - 1, mine], 0, off))
        everything.append(halves[-1])
        everything += lists[-1]

    queries[0, me_cell] = buffer[me_cell]
    away_in[me_cell] = away_out[me_cell]
    spread_out = []

    def forward(off):
        if off:
            for copy in routed[off]:
                copy.wait_recv()
        source = lax.rem(me_cell + groups - off, groups)
        for sub_off in range(1, shares):
            spread_out.append(
                send(queries.at[0, source], queries.at[sub_off, source], 0, sub_off)
            )

    forward(0)
    squares[...] = jnp.zeros_like(squares)

    @pl.loop(0, rows // step)
    def _(n):
        lanes = pl.ds(pl.multiple_of(n * step, step), step)
        cell_of = lax.rem(iota((LANES, step), 0), cells)
        shift = iota((LANES, step), 1) + n * step - cell_of * row_local
        far = jnp.where((shift >= 0) & (shift < row_local), floor_score, 0.0).astype(BF16)
        vectors[shares * own_width :, lanes] = far

    waiting = sorted(range(1, groups), key=lambda off: min(off, groups - off))
    pauses = [0]

    def between():
        if pauses[0] and waiting:
            forward(waiting.pop(0))
        pauses[0] += 1

    for k in range(shares):
        if k == 1:
            for off in range(1, shares):
                halves[off].wait_recv()
                here = books_in.at[off - 1, mine]
                lists[off].append(send(here, here, 0, 0, beside))
                everything.append(lists[off][-1])
        if k:
            for copy in lists[k]:
                copy.wait_recv()
        centers = coarse_in.at[k - 1] if k else coarse_ref

        @pl.loop(0, rows // step)
        def _(n):
            lanes = pl.ds(pl.multiple_of(n * step, step), step)
            shift = iota((cells, step), 1) + n * step - iota((cells, step), 0) * row_local
            inside = ((shift >= 0) & (shift < row_local)).astype(F32).astype(BF16)
            spread[:, lanes] = lax.dot_general(
                centers[...], inside, (((0,), (0,)), ((), ())), preferred_element_type=F32
            ).astype(BF16)

        decode_share(
            between,
            subs,
            book_width,
            blocks,
            codes_in.at[k - 1] if k else codes_ref.at[me_sub],
            books_in.at[k - 1] if k else books_ref,
            k * own_width,
            ids,
            spread,
            vectors,
            squares,
        )
    while waiting:
        forward(waiting.pop(0))
    everything += spread_out

    offset = iota((cells, rows), 1) - iota((cells, rows), 0) * row_local
    inside = (offset >= 0) & (offset < row_local)
    reach = jnp.zeros((cells, 1), jnp.int32)
    for c in range(cells):
        reach = jnp.where(iota((cells, 1), 0) == c, lengths_ref[c], reach)
    live = jnp.sum(
        (inside & (offset + me_sub * row_local < reach)).astype(F32),
        axis=0,
        keepdims=True,
    )
    half_norm = 0.5 * jnp.sum(squares[...], axis=0, keepdims=True)
    squares[0:1, :] = jnp.where(live > 0.5, half_norm, -floor_score)
    for copy in spread_out:
        copy.wait_recv()
    folds = LANES // cells
    deep = CAP // folds
    lane_group = iota((groups, deep, LANES), 2) // cells
    packed = away_in[...].astype(F32)
    for b in range(folds):
        away[:, b * deep : (b + 1) * deep] = jnp.where(lane_group == b, packed, 0.0).astype(BF16)
    part_cap = CAP // HALVES
    part_total = total // HALVES

    def score(h):
        some = slice(h * part_cap, (h + 1) * part_cap)
        best[h] = jnp.full(best.shape[1:], 3.0 * floor_score, F32)
        joined[h] = jnp.concatenate(
            [queries[k, :, some].reshape(part_total, own_width) for k in range(shares)]
            + [away[:, some].reshape(part_total, LANES)],
            axis=1,
        )

        @pl.loop(0, rows // step)
        def _(n):
            lanes = pl.ds(pl.multiple_of(n * step, step), step)
            raw = jnp.dot(joined[h], vectors[:, lanes], preferred_element_type=F32)
            scores = (raw - squares[0:1, lanes]) * score_scale
            values[h, :, lanes] = scores
            top = best[h]
            for b in range(step // LANES):
                top = jnp.maximum(top, scores[:, b * LANES : (b + 1) * LANES])
            best[h] = top

        peak_row[h, 0] = jnp.broadcast_to(
            jnp.max(jnp.transpose(best[h]), axis=0, keepdims=True), (8, part_total)
        )
        return [
            send(peak_row.at[h, 0], peak_row.at[h, off], 0, off) for off in range(1, shares)
        ]

    def pool(h, tops):
        for copy in tops:
            copy.wait_recv()
        peak = jnp.max(peak_row[h], axis=0)
        best[h] = jnp.transpose(jnp.broadcast_to(peak[0:1], (LANES, part_total)))
        part[...] = jnp.zeros_like(part)
        masses[...] = jnp.zeros_like(masses)

        @pl.loop(0, rows // step)
        def _(n):
            lanes = pl.ds(pl.multiple_of(n * step, step), step)
            mass = masses[...]
            pieces = []
            for b in range(step // LANES):
                inner = pl.ds(pl.multiple_of(n * step + b * LANES, LANES), LANES)
                piece = jnp.exp(values[h, :, inner] - best[h]).astype(BF16)
                mass = mass + piece.astype(F32)
                pieces.append(piece)
            masses[...] = mass
            part[...] += jnp.dot(
                jnp.concatenate(pieces, axis=1),
                payload_ref[lanes, :],
                preferred_element_type=F32,
            )

        mass_row[h, 0] = jnp.broadcast_to(
            jnp.sum(jnp.transpose(masses[...]), axis=0, keepdims=True), (8, part_total)
        )
        sums = part[...].reshape(groups, part_cap, width)
        for t in range(shares):
            own = slice(t * own_columns, (t + 1) * own_columns)
            share_out[h, t] = jnp.concatenate(
                [sums[:, b * short : (b + 1) * short, own] for b in range(fold)], axis=2
            ).astype(share_out.dtype)
        shared = []
        for off in range(1, shares):
            target = lax.rem(me_sub + off, shares)
            shared.append(send(share_out.at[h, target], share_in.at[h, off - 1], 0, off))
            shared.append(send(mass_row.at[h, 0], mass_row.at[h, off], 0, off))
        return shared, peak

    def give_back(h, shared, peak):
        for copy in shared:
            copy.wait_recv()
        share = share_out[h, me_sub].astype(F32)
        for off in range(1, shares):
            share = share + share_in[h, off - 1].astype(F32)
        back_out[h] = share
        sent = []
        for off in range(1, groups):
            target = lax.rem(me_cell + off, groups)
            sent.append(send(back_out.at[h, target], back_in.at[h, me_cell], off, 0))
        back_in[h, me_cell] = back_out[h, me_cell]
        mass_all = mass_row[h, 0]
        for off in range(1, shares):
            mass_all = mass_all + mass_row[h, off]
        return sent, jnp.where(iota((8, part_total), 0) == 0, mass_all, peak)

    tops = [score(h) for h in range(HALVES)]
    table_copy.wait()
    pooled = [pool(h, tops[h]) for h in range(HALVES)]
    given = [give_back(h, *pooled[h]) for h in range(HALVES)]
    returned = []
    for h in range(HALVES):
        everything += tops[h] + pooled[h][0] + given[h][0]
        returned += given[h][0]
    for g in range(groups):
        mine = [stats[:, g * part_cap : (g + 1) * part_cap] for _, stats in given]
        stat_out[g] = jnp.concatenate(mine + [jnp.zeros((8, LANES - CAP), F32)], axis=1)
    stat_sent = []
    for off in range(1, groups):
        target = lax.rem(me_cell + off, groups)
        stat_sent.append(send(stat_out.at[target], stat_in.at[me_cell], off, 0))
    everything += stat_sent
    returned += stat_sent
    stat_in[me_cell] = stat_out[me_cell]

    first, second, _, earlier = positions(meta_ref, groups)
    marks = []
    for route, named in ((0, first), (1, second)):
        spot = jnp.sum(
            named * earlier, axis=0, keepdims=True
        ).astype(jnp.int32)
        slot = meta_ref[route : route + 1, :] * CAP + spot
        marks.append((iota((total, count), 0) == slot).astype(F32).astype(BF16))
    for copy in returned:
        copy.wait_recv()

    def pick(array, mark, dim):
        out = 0.0
        for _ in range(3):
            piece = array.astype(BF16)
            out = out + lax.dot_general(
                piece, mark, (((dim,), (0,)), ((), ())), preferred_element_type=F32
            )
            array = array - piece.astype(F32)
        return out

    table = jnp.concatenate(
        [
            back_in[h][:, :, b * own_columns : (b + 1) * own_columns]
            for h in range(HALVES)
            for b in range(fold)
        ],
        axis=1,
    ).reshape(total, own_columns)
    stat_row = jnp.concatenate([stat_in[g][:, :CAP] for g in range(groups)], axis=1)
    stat_0, stat_1 = pick(stat_row, marks[0], 1), pick(stat_row, marks[1], 1)
    top = jnp.maximum(stat_0[1:2], stat_1[1:2])
    scale_0, scale_1 = jnp.exp(stat_0[1:2] - top), jnp.exp(stat_1[1:2] - top)
    lower = scale_0 * stat_0[0:1] + scale_1 * stat_1[0:1]
    upper = scale_0 * pick(table, marks[0], 0) + scale_1 * pick(table, marks[1], 0)
    columns[me_sub] = (upper / lower).astype(BF16)
    gathered = [
        send(columns.at[me_sub], columns.at[me_sub], 0, off) for off in range(1, shares)
    ]
    everything += gathered
    for copy in gathered:
        copy.wait_recv()
    pooled_ref[...] = columns[...].reshape(width, count)
    for copy in everything:
        copy.wait_send()


def local(queries, probe_groups, probe_cells, coarse, codebooks, codes, lengths, payload):
    groups, shares = lax.axis_size("cell"), lax.axis_size("sub")
    count, own_width = queries.shape
    half = probe_cells.shape[2]
    cells, own_subs, row_slots = codes.shape
    row_local = row_slots // shares
    rows = cells * row_local
    total = groups * CAP
    width = payload.shape[2]
    fold = LANES // (width // shares)
    short = CAP // fold // HALVES
    meta = jnp.concatenate([probe_groups, probe_cells.reshape(count, -1)], axis=1).T
    copies = (3 + HALVES) * (groups - 1) + (groups + 5 + 3 * HALVES) * (shares - 1)
    spec = pl.BlockSpec(memory_space=pltpu.VMEM)
    pooled = pl.pallas_call(
        functools.partial(whole_kernel, groups, shares, half, row_local, fold),
        out_shape=jax.ShapeDtypeStruct((width, count), BF16),
        in_specs=[spec] * 5 + [pl.BlockSpec(memory_space=pltpu.SMEM), pl.BlockSpec(memory_space=pl.ANY)],
        out_specs=spec,
        scratch_shapes=[
            pltpu.VMEM((rows, width), BF16),
            pltpu.SemaphoreType.DMA,
            pltpu.VMEM((shares, own_subs, rows), BF16),
            pltpu.VMEM((groups, CAP, own_width), BF16),
            pltpu.VMEM((groups, CAP * cells // LANES, LANES), BF16),
            pltpu.VMEM((shares, groups, CAP, own_width), BF16),
            pltpu.VMEM((groups, CAP * cells // LANES, LANES), BF16),
            pltpu.VMEM((groups, CAP, LANES), BF16),
            pltpu.VMEM((shares - 1, own_subs, rows), BF16),
            pltpu.VMEM((shares - 1,) + codebooks.shape, BF16),
            pltpu.VMEM((shares - 1,) + coarse.shape, BF16),
            pltpu.VMEM((own_subs, rows), jnp.int32),
            pltpu.VMEM((own_width, rows), BF16),
            pltpu.VMEM((HALVES, total // HALVES, shares * own_width + LANES), BF16),
            pltpu.VMEM((shares * own_width + LANES, rows), BF16),
            pltpu.VMEM((8, rows), F32),
            pltpu.VMEM((HALVES, total // HALVES, LANES), F32),
            pltpu.VMEM((HALVES, total // HALVES, rows), F32),
            pltpu.VMEM((HALVES, shares, 8, total // HALVES), F32),
            pltpu.VMEM((total // HALVES, width), F32),
            pltpu.VMEM((total // HALVES, LANES), F32),
            pltpu.VMEM((HALVES, shares, 8, total // HALVES), F32),
            pltpu.VMEM((HALVES, shares, groups, short, LANES), F32),
            pltpu.VMEM((HALVES, shares - 1, groups, short, LANES), F32),
            pltpu.VMEM((HALVES, groups, short, LANES), F32),
            pltpu.VMEM((HALVES, groups, short, LANES), F32),
            pltpu.VMEM((groups, 8, LANES), F32),
            pltpu.VMEM((groups, 8, LANES), F32),
            pltpu.VMEM((shares, width // shares, count), BF16),
            pltpu.SemaphoreType.DMA((copies,)),
            pltpu.SemaphoreType.DMA((copies,)),
        ],
        compiler_params=pltpu.CompilerParams(
            collective_id=0, has_side_effects=True, vmem_limit_bytes=56 * 1024 * 1024
        ),
    )(meta, queries, codes, codebooks, coarse, lengths, payload.reshape(rows, width))
    return pooled.T


def solution(mesh):
    placed = (
        P("cell", "sub"),
        P("cell", None),
        P("cell", None, None),
        P("cell", "sub"),
        P("sub", None, None),
        P("cell", "sub", None),
        P("cell"),
        P("cell", "sub", None),
    )
    return jax.shard_map(
        local, mesh=mesh, in_specs=placed, out_specs=P("cell", None), check_vma=False
    )
```
